256 devices in a mesh: tm: 8 (over x, core), node: 32 (over z, y).
Axes of the slice: x: 4, y: 4, z: 8, core: 2. Of those that a mesh axis runs over, the one named last changes fastest.
Arguments:
- memory: float32 [16384, 256], P('node'), may hold values from -6 to 6
- touched: int32 [8, 32, 256], P(None, 'node'), may hold values from 0 to 511, as said below
- src_slot: int32 [8, 32, 512], P('tm', 'node'), may hold values from 0 to 255, as said below
- ev_count: int32 [8, 32], P('tm', 'node'), may hold values from 256 to 512, as said below
- serve_rows: int32 [8, 32, 1024], P('tm', 'node'), may hold values from 0 to 511
- dst_slot: int32 [8, 32, 512], P('tm', 'node'), may hold values from 0 to 1023
- nbr_slot: int32 [8, 32, 10, 512], P('tm', 'node'), may hold values from 0 to 1023
- ev_gap: int32 [8, 32, 512], P('tm', 'node'), may hold values from 0 to 999
- nbr_gap: int32 [8, 32, 10, 512], P('tm', 'node'), may hold values from 1 to 999
- time_freq: float32 [100], replicated, may hold values from 0.001 to 0.1
- time_phase: float32 [100], replicated, may hold values from -3.140625 to 3.140625
- w_msg: bfloat16 [612, 256], replicated, may hold values from -0.25 to 0.25
- w_in: bfloat16 [256, 768], replicated, may hold values from -0.375 to 0.375
- w_hid: bfloat16 [256, 768], replicated, may hold values from -0.375 to 0.375
- w_nbr: bfloat16 [356, 256], replicated, may hold values from -0.09375 to 0.09375
- w_out: bfloat16 [512, 256], replicated, may hold values from -0.25 to 0.25
Outputs:
- embeddings: bfloat16 [8, 32, 512, 256], P('tm', 'node')
- memory_after: float32 [8, 16384, 256], P('tm', 'node')
The draws below stay inside these ranges and needn't reach their ends.
Inputs may be any that keep to these rules, and one draw needn't show every extreme that they name: `touched`: for every segment and shard the 256 rows are distinct local rows. `src_slot`: the first 256 events of each segment and shard name every touched position exactly once. `ev_count`: in every segment some shard has all 512 event slots live.
All inputs are finite; a program needn't handle non-finite values.
Results may differ from the reference program's by a relative error of at most 0.015.
Values may be sent and summed in bfloat16 or wider, within the bound.
No kernel may reach another device: no remote copies, remote signals or barrier semaphores. Data moves between devices by JAX's collectives and lax.ppermute only.
A program may use at most 128 MiB of HBM per device.

```python
import math
import jax
import jax.numpy as jnp

DM = 256
TD = 100
NBRS = 10
ROWS = 512
EV = 512
CAP = 32
TOUCH = 256
SEG = 8
SHARDS = 32
NODES = 16384


def distinct_order(key, count, length):
    scores = jax.random.randint(key, (SEG, SHARDS, length), 0, 4096) * length + jnp.arange(length, dtype=jnp.int32)
    return jnp.argsort(scores, axis=-1)[..., :count].astype(jnp.int32)


def draw_touched(key, part):
    key = jax.random.fold_in(key, 11)
    return distinct_order(key, TOUCH, ROWS)


def draw_src_slot(key, part):
    key = jax.random.fold_in(key, 12)
    first_key, rest_key = jax.random.split(key)
    leading = distinct_order(first_key, TOUCH, TOUCH)
    trailing = jax.random.randint(rest_key, (SEG, SHARDS, EV - TOUCH), 0, TOUCH)
    return jnp.concatenate([leading, trailing], axis=2).astype(jnp.int32)


def draw_ev_count(key, part):
    key = jax.random.fold_in(key, 13)
    count_key, full_key = jax.random.split(key)
    counts = jax.random.randint(count_key, (SEG, SHARDS), TOUCH, EV + 1)
    fullest = jax.random.randint(full_key, (SEG, 1), 0, SHARDS)
    return jnp.where(jnp.arange(SHARDS)[None, :] == fullest, EV, counts).astype(jnp.int32)


def plant(values, rng, smallest, high):
    place = [jax.random.randint(jax.random.fold_in(rng, axis), (), 0, length) for axis, length in enumerate(values.shape)]
    longest = values.shape.index(max(values.shape))
    beside = place[:longest] + [(place[longest] + 1) % values.shape[longest]] + place[longest + 1:]
    return values.at[tuple(place)].set(smallest).at[tuple(beside)].set(high)


def steps_of(rng, extent, cuts, low, largest):
    loudness = 1.0
    for position, shards_of in cuts:
        heights = jax.random.uniform(jax.random.fold_in(jax.random.fold_in(rng, 6), position), (shards_of,), jnp.float32, low / len(cuts), largest / len(cuts))
        loudness = loudness * jnp.repeat(jnp.exp(heights), extent[position] // shards_of).reshape((-1,) + (1,) * (len(extent) - 1 - position))
    return loudness


def gaussian(stream_key, dims, spread, most, pieces=(), held_as=jnp.bfloat16):
    loudness = steps_of(stream_key, dims, pieces, -0.22, 0.18) if pieces else 1.0
    array = jax.random.normal(stream_key, dims, jnp.float32) * spread * loudness
    return jnp.minimum(jnp.maximum(array, -most), most).astype(held_as)


def setup_inputs(seed: int = 0) -> dict:
    splits = jax.random.split(jax.random.key(seed), 17)
    return {
        "memory": gaussian(splits[0], (NODES, DM), 1.0, 6.0, ((0, 32),), jnp.float32),
        "touched": draw_touched(jax.random.fold_in(splits[16], 71), 0),
        "src_slot": draw_src_slot(jax.random.fold_in(splits[16], 71), 0),
        "ev_count": draw_ev_count(jax.random.fold_in(splits[16], 71), 0),
        "serve_rows": plant(jax.random.randint(splits[4], (SEG, SHARDS, SHARDS * CAP), 0, ROWS), jax.random.fold_in(splits[4], 1), 0, ROWS - 1).astype(jnp.int32),
        "dst_slot": plant(jax.random.randint(splits[5], (SEG, SHARDS, EV), 0, SHARDS * CAP), jax.random.fold_in(splits[5], 1), 0, (SHARDS * CAP) - 1).astype(jnp.int32),
        "nbr_slot": plant(jax.random.randint(splits[6], (SEG, SHARDS, NBRS, EV), 0, SHARDS * CAP), jax.random.fold_in(splits[6], 1), 0, (SHARDS * CAP) - 1).astype(jnp.int32),
        "ev_gap": plant(jax.random.randint(splits[7], (SEG, SHARDS, EV), 0, 1000), jax.random.fold_in(splits[7], 1), 0, 999).astype(jnp.int32),
        "nbr_gap": plant(jax.random.randint(splits[8], (SEG, SHARDS, NBRS, EV), 1, 1000), jax.random.fold_in(splits[8], 1), 1, 999).astype(jnp.int32),
        "time_freq": jnp.clip(jnp.exp(jax.random.uniform(splits[9], (TD,), jnp.float32, math.log(0.001), math.log(0.1))), 0.001, 0.1),
        "time_phase": jnp.clip(jax.random.uniform(splits[10], (TD,), jnp.float32, -3.140625, 3.140625), -3.140625, 3.140625),
        "w_msg": gaussian(splits[11], (2 * DM + TD, DM), (2 * DM + TD) ** -0.5, 0.25),
        "w_in": gaussian(splits[12], (DM, 3 * DM), DM ** -0.5, 0.375),
        "w_hid": gaussian(splits[13], (DM, 3 * DM), DM ** -0.5, 0.375),
        "w_nbr": gaussian(splits[14], (DM + TD, DM), (NBRS * (DM + TD)) ** -0.5, 0.09375),
        "w_out": gaussian(splits[15], (2 * DM, DM), (2 * DM) ** -0.5, 0.25),
    }


def time_code(ticks, time_freq, time_phase):
    return jnp.cos(ticks.astype(jnp.float32)[..., None] * time_freq + time_phase)


def gru_rows(inputs_b, hidden_f, w_in, w_hid):
    input_gates = jnp.dot(inputs_b, w_in, preferred_element_type=jnp.float32)
    hidden_gates = jnp.dot(hidden_f.astype(jnp.bfloat16), w_hid, preferred_element_type=jnp.float32)
    reset_gate = jax.nn.sigmoid(input_gates[:, :DM] + hidden_gates[:, :DM])
    update_gate = jax.nn.sigmoid(input_gates[:, DM:2 * DM] + hidden_gates[:, DM:2 * DM])
    candidate = jnp.tanh(input_gates[:, 2 * DM:] + reset_gate * hidden_gates[:, 2 * DM:])
    return (1.0 - update_gate) * candidate + update_gate * hidden_f


def reference(memory, touched, src_slot, ev_count, serve_rows, dst_slot, nbr_slot, ev_gap, nbr_gap, time_freq, time_phase, w_msg, w_in, w_hid, w_nbr, w_out):
    offsets = jnp.arange(SHARDS, dtype=jnp.int32) * ROWS
    positions = jnp.arange(EV, dtype=jnp.int32)
    slot_ids = jnp.arange(TOUCH, dtype=jnp.int32)
    memory_now = memory
    embed_list = []
    snapshots = []
    for segment in range(SEG):
        memory_b = memory_now.astype(jnp.bfloat16)
        served = serve_rows[segment].reshape(SHARDS, SHARDS, CAP) + offsets[:, None, None]
        fetch_index = jnp.transpose(served, (1, 0, 2)).reshape(SHARDS, SHARDS * CAP)
        fetched = memory_b[fetch_index]
        touch_rows = touched[segment] + offsets[:, None]
        held_rows = memory_now[touch_rows]
        src_rows = jax.vmap(lambda table, picks: table[picks])(held_rows.astype(jnp.bfloat16), src_slot[segment])
        dst_rows = jax.vmap(lambda table, picks: table[picks])(fetched, dst_slot[segment])
        live_mask = (positions[None, :] < ev_count[segment][:, None]).astype(jnp.float32)
        ev_code = time_code(ev_gap[segment], time_freq, time_phase).astype(jnp.bfloat16)
        msg_in = jnp.concatenate([src_rows, dst_rows, ev_code], axis=2).reshape(SHARDS * EV, 2 * DM + TD)
        messages = jnp.dot(msg_in, w_msg, preferred_element_type=jnp.float32).astype(jnp.bfloat16).reshape(SHARDS, EV, DM)
        member = (slot_ids[None, :, None] == src_slot[segment][:, None, :]).astype(jnp.float32) * live_mask[:, None, :]
        counts = jnp.sum(member, axis=2)
        totals = jnp.einsum("ste,sed->std", member, messages.astype(jnp.float32))
        aggregate = (totals / counts[:, :, None]).astype(jnp.bfloat16)
        fresh_rows = gru_rows(aggregate.reshape(SHARDS * TOUCH, DM), held_rows.reshape(SHARDS * TOUCH, DM), w_in, w_hid)
        memory_now = memory_now.at[touch_rows.reshape(-1)].set(fresh_rows)
        fresh_b = fresh_rows.astype(jnp.bfloat16).reshape(SHARDS, TOUCH, DM)
        src_new = jax.vmap(lambda table, picks: table[picks])(fresh_b, src_slot[segment])
        nbr_rows = jax.vmap(lambda table, picks: table[picks])(fetched, nbr_slot[segment])
        nbr_sum = jnp.sum(nbr_rows.astype(jnp.float32), axis=1)
        nbr_codes = jnp.sum(time_code(nbr_gap[segment], time_freq, time_phase), axis=1)
        nbr_in = jnp.concatenate([nbr_sum, nbr_codes], axis=2).astype(jnp.bfloat16).reshape(SHARDS * EV, DM + TD)
        hidden_b = jax.nn.relu(jnp.dot(nbr_in, w_nbr, preferred_element_type=jnp.float32)).astype(jnp.bfloat16)
        joined = jnp.concatenate([src_new.reshape(SHARDS * EV, DM), hidden_b], axis=1)
        embedded = jnp.dot(joined, w_out, preferred_element_type=jnp.float32).reshape(SHARDS, EV, DM) * live_mask[:, :, None]
        embed_list.append(embedded.astype(jnp.bfloat16))
        snapshots.append(memory_now)
    return jnp.stack(embed_list), jnp.stack(snapshots)
```

```python
import functools

import jax
import jax.numpy as jnp
from jax import lax
from jax.experimental import pallas as pl
from jax.experimental.pallas import tpu as pltpu
from jax.sharding import PartitionSpec as P

DM = 256
TD = 100
CODE = 128
F32 = jnp.float32
BF16 = jnp.bfloat16
VMEM = pl.BlockSpec(memory_space=pltpu.VMEM)
SMEM = pl.BlockSpec(memory_space=pltpu.SMEM)
ANY = pl.BlockSpec(memory_space=pl.ANY)


def dot(a, b):
    return jnp.dot(a, b, preferred_element_type=F32)


def dot_nt(a, b):
    return lax.dot_general(a, b, (((1,), (1,)), ((), ())), preferred_element_type=F32)


def iota(shape, axis):
    return lax.broadcasted_iota(jnp.int32, shape, axis)


def ones_where(mask):
    return jnp.where(mask, 1.0, 0.0).astype(BF16)


def split_two(x):
    high = x.astype(BF16)
    return high, (x - high.astype(F32)).astype(BF16)


def hit_rows(place):
    return jnp.max(place.astype(F32), axis=1, keepdims=True) > 0.5


def pack_kernel(serve_ref, dst_ref, src_ref, gap_ref, count_ref, out_ref):
    for i in range(out_ref.shape[0]):
        at = 0
        for ref in (serve_ref, dst_ref, src_ref, gap_ref):
            out_ref[i, at : at + ref.shape[0], :] = ref[...]
            at += ref.shape[0]
        out_ref[i, at:, :] = jnp.full((out_ref.shape[1] - at, 128), count_ref[0, 0], jnp.int32)


def first_serve_kernel(serve_ref, memory_ref, out_ref):
    rows = memory_ref.shape[0]
    pick = ones_where(serve_ref[:, 0:1] == iota((serve_ref.shape[0], rows), 1))
    out_ref[...] = dot(pick, memory_ref[...].astype(BF16)).astype(BF16)


def prepare_kernel(
    turn,
    last,
    me_ref,
    memory_ref,
    fresh_ref,
    touched_ref,
    touched_t_ref,
    src_ref,
    dst_ref,
    gap_ref,
    count_ref,
    serve_t_ref,
    freq_ref,
    phase_ref,
    w_src_ref,
    w_code_ref,
    w_hid_ref,
    snap_in_ref,
    memory_out,
    held_out,
    gh_out,
    links_out,
    inv_out,
    base_out,
    static_out,
    snap_out,
    sem,
):
    rows = memory_ref.shape[0]
    touch = touched_ref.shape[1]
    events = src_ref.shape[1]
    slots = links_out.shape[1]
    if turn > 0:
        place = ones_where(iota((rows, touch), 0) == touched_ref[turn - 1 : turn, :])
        high, low = split_two(fresh_ref[...])
        memory = jnp.where(hit_rows(place), dot(place, high) + dot(place, low), memory_ref[...])
    else:
        memory = memory_ref[...]
    memory_out[...] = memory
    if turn > 0:

        @pl.when(me_ref[0] == turn - 1)
        def _():
            copy = pltpu.make_async_copy(memory_out, snap_out, sem)
            copy.start()
            copy.wait()

    memory_b, memory_low = split_two(memory)
    pick = ones_where(touched_t_ref[:, turn : turn + 1] == iota((touch, rows), 1))
    held_b = dot(pick, memory_b)
    held_out[...] = held_b + dot(pick, memory_low)
    held_b = held_b.astype(BF16)
    gh_out[...] = dot(held_b, w_hid_ref[...])
    live = iota((touch, events), 1) < count_ref[turn]
    member_mask = jnp.logical_and(iota((touch, events), 0) == src_ref[turn : turn + 1, :], live)
    member_f = jnp.where(member_mask, 1.0, 0.0)
    member = member_f.astype(BF16)
    inv = 1.0 / jnp.sum(member_f, axis=1, keepdims=True)
    inv_out[...] = inv
    dst_pick = ones_where(iota((slots, events), 0) == dst_ref[turn : turn + 1, :])
    links_out[...] = dot_nt(member, dst_pick).astype(BF16)
    angle = freq_ref[...] * gap_ref[turn : turn + 1, :].astype(F32) + phase_ref[...]
    code = jnp.cos(angle).astype(BF16)
    code_mean = (dot_nt(member, code) * inv).astype(BF16)
    base_out[...] = dot(held_b, w_src_ref[...]) + dot(code_mean, w_code_ref[...])
    if not last:
        kept_place = ones_where(iota((rows, touch), 0) == touched_ref[turn : turn + 1, :])
        kept = jnp.where(hit_rows(kept_place), 0.0, memory).astype(BF16)
        serve = ones_where(
            serve_t_ref[:, turn + 1 : turn + 2] == iota((serve_t_ref.shape[0], rows), 1)
        )
        static_out[...] = dot(serve, kept).astype(BF16)


def update_kernel(
    turn,
    last,
    own_ref,
    other_ref,
    links_ref,
    inv_ref,
    base_ref,
    gh_ref,
    held_ref,
    static_ref,
    serve_t_ref,
    touched_ref,
    w_dst_ref,
    w_in_ref,
    fresh_out,
    served_out,
):
    half = own_ref.shape[0]
    raw = dot(links_ref[:, :half], own_ref[...]) + dot(links_ref[:, half:], other_ref[...])
    raw = (raw * inv_ref[...]).astype(BF16)
    aggregate = (dot(raw, w_dst_ref[...]) + base_ref[...]).astype(BF16)
    gi = dot(aggregate, w_in_ref[...])
    gh = gh_ref[...]
    reset_gate = jax.nn.sigmoid(gi[:, :DM] + gh[:, :DM])
    update_gate = jax.nn.sigmoid(gi[:, DM : 2 * DM] + gh[:, DM : 2 * DM])
    candidate = jnp.tanh(gi[:, 2 * DM :] + reset_gate * gh[:, 2 * DM :])
    fresh = (1.0 - update_gate) * candidate + update_gate * held_ref[...]
    fresh_out[...] = fresh
    if not last:
        hits = ones_where(
            serve_t_ref[:, turn + 1 : turn + 2] == touched_ref[turn : turn + 1, :]
        )
        served = dot(hits, fresh.astype(BF16)) + static_ref[...].astype(F32)
        served_out[...] = served.astype(BF16)


def neighbours_kernel(nbr_ref, out_ref):
    events, slots = out_ref.shape
    block = 64

    def step(i, carry):
        at = pl.ds(pl.multiple_of(i * block, block), block)
        picks = nbr_ref[at, :]
        lanes = iota((block, slots), 1)
        total = jnp.zeros((block, slots), F32)
        for q in range(nbr_ref.shape[1]):
            total += jnp.where(picks[:, q : q + 1] == lanes, 1.0, 0.0)
        out_ref[at, :] = total.astype(BF16)
        return carry

    lax.fori_loop(0, events // block, step, 0)


def embed_kernel(
    turn,
    me_ref,
    fresh_ref,
    own_ref,
    other_ref,
    nbr_ref,
    codes_ref,
    src_t_ref,
    count_ref,
    w_nbr_ref,
    w_nbr_code_ref,
    w_out_ref,
    emb_in_ref,
    emb_out,
    emb_scr,
    sem,
):
    @pl.when(me_ref[0] == turn)
    def _():
        events = emb_scr.shape[0]
        half = own_ref.shape[0]
        near = dot(nbr_ref[:, :half], own_ref[...]) + dot(nbr_ref[:, half:], other_ref[...])
        hidden = dot(near.astype(BF16), w_nbr_ref[...]) + dot(codes_ref[...], w_nbr_code_ref[...])
        hidden = jnp.maximum(hidden, 0.0).astype(BF16)
        src_pick = ones_where(src_t_ref[...] == iota((events, fresh_ref.shape[0]), 1))
        src_new = dot(src_pick, fresh_ref[...].astype(BF16)).astype(BF16)
        out = dot(src_new, w_out_ref[:DM, :]) + dot(hidden, w_out_ref[DM:, :])
        live = iota((events, 1), 0) < count_ref[turn]
        emb_scr[...] = jnp.where(live, out, 0.0).astype(BF16)
        copy = pltpu.make_async_copy(emb_scr, emb_out, sem)
        copy.start()
        copy.wait()


def finish_kernel(turn, me_ref, memory_ref, fresh_ref, touched_ref, snap_in_ref, snap_out, scr, sem):
    @pl.when(me_ref[0] == turn)
    def _():
        rows, touch = memory_ref.shape[0], touched_ref.shape[1]
        place = ones_where(iota((rows, touch), 0) == touched_ref[turn : turn + 1, :])
        high, low = split_two(fresh_ref[...])
        scr[...] = jnp.where(hit_rows(place), dot(place, high) + dot(place, low), memory_ref[...])
        copy = pltpu.make_async_copy(scr, snap_out, sem)
        copy.start()
        copy.wait()


def shape(dims, dtype):
    return jax.ShapeDtypeStruct(dims, dtype)


def params():
    return pltpu.CompilerParams(vmem_limit_bytes=24 * 1024 * 1024)


def cost(flops, bytes_accessed):
    return pl.CostEstimate(flops=flops, bytes_accessed=bytes_accessed, transcendentals=0)


def body(
    memory,
    touched,
    src_slot,
    ev_count,
    serve_rows,
    dst_slot,
    nbr_slot,
    ev_gap,
    nbr_gap,
    time_freq,
    time_phase,
    w_msg,
    w_in,
    w_hid,
    w_nbr,
    w_out,
):
    me = lax.axis_index("tm")
    core = me % 2
    sections = lax.axis_size("tm")
    shards = lax.axis_size("node")
    rows = memory.shape[0]
    events = src_slot.shape[2]
    slots = serve_rows.shape[2]
    half = slots // 2
    capacity = slots // shards
    part = capacity // 2
    touched = touched[:, 0, :]
    touch = touched.shape[1]

    lists = [
        serve_rows.reshape(-1, 128),
        dst_slot.reshape(-1, 128),
        src_slot.reshape(-1, 128),
        ev_gap.reshape(-1, 128),
    ]
    lines = sum(x.shape[0] for x in lists) + 4
    packed = pl.pallas_call(
        pack_kernel,
        out_shape=shape((sections, lines, 128), jnp.int32),
        in_specs=[VMEM] * 4 + [SMEM],
        out_specs=VMEM,
        compiler_params=params(),
        name="pack",
    )(*lists, ev_count)
    everyone = lax.all_to_all(packed, "tm", split_axis=0, concat_axis=0, tiled=True).reshape(
        sections, -1
    )
    serve_all = everyone[:, :slots].reshape(sections, shards, 2, part)
    serve_own = jnp.where(core == 0, serve_all[:, :, 0], serve_all[:, :, 1])
    serve_t = serve_own.reshape(sections, half).T
    at = slots
    dst_all = everyone[:, at : at + events]
    at += events
    src_all = everyone[:, at : at + events]
    at += events
    gap_all = everyone[:, at : at + events]
    at += events
    count_all = everyone[:, at]

    def reordered(slot):
        place = slot % capacity
        mine = (place // part) == core
        return (slot // capacity) * part + place % part + jnp.where(mine, 0, half)

    dst_all = reordered(dst_all)
    touched_t = touched.T
    me_s = me.reshape(1).astype(jnp.int32)
    freq = jnp.pad(time_freq, (0, CODE - TD)).reshape(CODE, 1)
    phase = jnp.pad(time_phase, (0, CODE - TD)).reshape(CODE, 1)
    w_src, w_dst, w_code = w_msg[:DM], w_msg[DM : 2 * DM], w_msg[2 * DM :]
    w_code = jnp.pad(w_code, ((0, CODE - TD), (0, 0)))
    w_nbr_code = jnp.pad(w_nbr[DM:], ((0, CODE - TD), (0, 0)))
    w_nbr_row = w_nbr[:DM]

    served = pl.pallas_call(
        first_serve_kernel,
        out_shape=shape((half, DM), BF16),
        in_specs=[VMEM] * 2,
        out_specs=VMEM,
        compiler_params=params(),
        name="first_serve",
    )(serve_t, memory)

    nbr_t = reordered(nbr_slot[0, 0]).T
    nbr_counts = pl.pallas_call(
        neighbours_kernel,
        out_shape=shape((events, slots), BF16),
        in_specs=[VMEM],
        out_specs=VMEM,
        compiler_params=params(),
        cost_estimate=cost(10**9, 2**20),
        name="neighbour_counts",
    )(nbr_t)
    nbr_angles = nbr_gap[0, 0].astype(F32)[..., None] * jnp.pad(time_freq, (0, CODE - TD)) + jnp.pad(
        time_phase, (0, CODE - TD)
    )
    nbr_codes = jnp.sum(jnp.cos(nbr_angles), axis=0).astype(BF16)
    src_t = src_slot.reshape(events, 1)

    done = []

    def run_embed(before, emb):
        return embed(
            before,
            me_s,
            *done[before],
            nbr_counts,
            nbr_codes,
            src_t,
            count_all,
            w_nbr_row,
            w_nbr_code,
            w_out,
            emb,
        )

    emb = jnp.zeros((events, DM), BF16)
    snap = jnp.zeros((rows, DM), F32)
    memory_now = memory
    fresh = jnp.zeros((touch, DM), F32)
    swap = [(i, i ^ 1) for i in range(sections)]
    for turn in range(sections):
        last = turn + 1 == sections
        own = lax.all_to_all(
            served.reshape(shards, part, DM), "node", split_axis=0, concat_axis=0, tiled=True
        ).reshape(half, DM)
        memory_now, held, gh, links, inv, base, static, snap = pl.pallas_call(
            functools.partial(prepare_kernel, turn, last),
            out_shape=(
                shape((rows, DM), F32),
                shape((touch, DM), F32),
                shape((touch, 3 * DM), F32),
                shape((touch, slots), BF16),
                shape((touch, 1), F32),
                shape((touch, DM), F32),
                shape((half, DM), BF16),
                shape((rows, DM), F32),
            ),
            in_specs=[SMEM] + [VMEM] * 7 + [SMEM] + [VMEM] * 6 + [ANY],
            out_specs=(VMEM,) * 7 + (ANY,),
            scratch_shapes=[pltpu.SemaphoreType.DMA],
            input_output_aliases={15: 7},
            compiler_params=params(),
            cost_estimate=cost(2 * 10**9, 2**22),
            name="prepare",
        )(
            me_s,
            memory_now,
            fresh,
            touched,
            touched_t,
            src_all,
            dst_all,
            gap_all,
            count_all,
            serve_t,
            freq,
            phase,
            w_src,
            w_code,
            w_hid,
            snap,
        )
        ready = () if turn < 2 else ((0, 1) if turn == 2 else (turn - 1,))
        for before in ready:
            emb = run_embed(before, emb)
        tied = (own, memory_now, held, gh, links, inv, base, static, snap, emb)
        if turn == 0:
            tied = tied + (nbr_counts,)
        if turn == 1:
            tied = tied + (nbr_codes,)
        tied = lax.optimization_barrier(tied)
        own, memory_now, held, gh, links, inv, base, static, snap, emb = tied[:10]
        if turn == 0:
            nbr_counts = tied[10]
        if turn == 1:
            nbr_codes = tied[10]
        other = lax.ppermute(own, "tm", swap)
        fresh, served = pl.pallas_call(
            functools.partial(update_kernel, turn, last),
            out_shape=(shape((touch, DM), F32), shape((half, DM), BF16)),
            in_specs=[VMEM] * 12,
            out_specs=(VMEM,) * 2,
            compiler_params=params(),
            cost_estimate=cost(10**9, 2**22),
            name="update",
        )(
            own,
            other,
            links,
            inv,
            base,
            gh,
            held,
            static,
            serve_t,
            touched,
            w_dst,
            w_in,
        )
        done.append((fresh, own, other))
    emb = run_embed(turn, emb)
    snap = pl.pallas_call(
        functools.partial(finish_kernel, turn),
        out_shape=shape((rows, DM), F32),
        in_specs=[SMEM] + [VMEM] * 3 + [ANY],
        out_specs=ANY,
        scratch_shapes=[pltpu.VMEM((rows, DM), F32), pltpu.SemaphoreType.DMA],
        input_output_aliases={4: 0},
        compiler_params=params(),
        name="finish",
    )(me_s, memory_now, fresh, touched, snap)
    return (emb[None, None], snap[None])


def embed(turn, me_s, fresh, own, other, nbr_counts, nbr_codes, src_t, count_all, w_nbr_row, w_nbr_code, w_out, emb):
    events = emb.shape[0]
    return pl.pallas_call(
        functools.partial(embed_kernel, turn),
        out_shape=shape((events, DM), BF16),
        in_specs=[SMEM] + [VMEM] * 6 + [SMEM] + [VMEM] * 3 + [ANY],
        out_specs=ANY,
        scratch_shapes=[pltpu.VMEM((events, DM), BF16), pltpu.SemaphoreType.DMA],
        input_output_aliases={11: 0},
        compiler_params=params(),
        cost_estimate=cost(10**9, 2**22),
        name="embed",
    )(me_s, fresh, own, other, nbr_counts, nbr_codes, src_t, count_all, w_nbr_row, w_nbr_code, w_out, emb)


def solution(mesh):
    return jax.shard_map(
        body,
        mesh=mesh,
        in_specs=(
            P("node", None),
            P(None, "node", None),
            P("tm", "node", None),
            P("tm", "node"),
            P("tm", "node", None),
            P("tm", "node", None),
            P("tm", "node", None, None),
            P("tm", "node", None),
            P("tm", "node", None, None),
            P(),
            P(),
            P(),
            P(),
            P(),
            P(),
            P(),
        ),
        out_specs=(P("tm", "node", None, None), P("tm", "node", None)),
        check_vma=False,
    )
```

```python
import functools

import jax
import jax.numpy as jnp
from jax import lax
from jax.experimental import pallas as pl
from jax.experimental.pallas import tpu as pltpu
from jax.sharding import PartitionSpec as P

DM = 256
TD = 100
CODE = 128
F32 = jnp.float32
BF16 = jnp.bfloat16
VMEM = pl.BlockSpec(memory_space=pltpu.VMEM)
SMEM = pl.BlockSpec(memory_space=pltpu.SMEM)
ANY = pl.BlockSpec(memory_space=pl.ANY)
HBM = pl.BlockSpec(memory_space=pltpu.HBM)


def dot(a, b):
    return jnp.dot(a, b, preferred_element_type=F32)


def dot_nt(a, b):
    return lax.dot_general(a, b, (((1,), (1,)), ((), ())), preferred_element_type=F32)


def iota(shape, axis):
    return lax.broadcasted_iota(jnp.int32, shape, axis)


def ones_where(mask):
    return jnp.where(mask, 1.0, 0.0).astype(BF16)


def split_two(x):
    high = x.astype(BF16)
    return high, (x - high.astype(F32)).astype(BF16)


def hit_rows(place):
    return jnp.max(place.astype(F32), axis=1, keepdims=True) > 0.5


def copies(pairs, sems):
    return [pltpu.make_async_copy(src, dst, sems.at[i]) for i, (src, dst) in enumerate(pairs)]


def pack_kernel(serve_ref, dst_ref, src_ref, gap_ref, count_ref, out_ref, scr, in_sems, out_sems):
    at, pairs = 0, []
    for ref in (serve_ref, dst_ref, src_ref, gap_ref):
        pairs.append((ref, scr.at[at : at + ref.shape[0]]))
        at += ref.shape[0]
    loads = copies(pairs, in_sems)
    for copy in loads:
        copy.start()
    scr[at:, :] = jnp.full((scr.shape[0] - at, 128), count_ref[0, 0], jnp.int32)
    for copy in loads:
        copy.wait()
    sends = copies([(scr, out_ref.at[i]) for i in range(out_ref.shape[0])], out_sems)
    for copy in sends:
        copy.start()
    for copy in sends:
        copy.wait()


def first_serve_kernel(serve_ref, memory_ref, out_ref):
    rows = memory_ref.shape[0]
    pick = ones_where(serve_ref[:, 0:1] == iota((serve_ref.shape[0], rows), 1))
    out_ref[...] = dot(pick, memory_ref[...].astype(BF16)).astype(BF16)


def prepare_kernel(
    turn,
    last,
    me_ref,
    memory_ref,
    fresh_ref,
    touched_ref,
    touched_t_ref,
    src_ref,
    dst_ref,
    gap_ref,
    count_ref,
    serve_t_ref,
    freq_ref,
    phase_ref,
    w_src_ref,
    w_code_ref,
    w_hid_ref,
    *rest,
):
    outs, scratch = rest[turn > 1 : (turn > 1) + 7], rest[-9:-2]
    snap_out = rest[-10]
    sems, snap_sem = rest[-2:]
    memory_scr, held_scr, gh_scr, links_scr, base_scr, static_scr, hits_scr = scratch
    rows = memory_ref.shape[0]
    touch = touched_ref.shape[1]
    events = src_ref.shape[1]
    slots = links_scr.shape[1]
    stores = copies(zip(scratch, outs), sems)
    if turn > 0:
        place = ones_where(iota((rows, touch), 0) == touched_ref[turn - 1 : turn, :])
        high, low = split_two(fresh_ref[...])
        memory = jnp.where(hit_rows(place), dot(place, high) + dot(place, low), memory_ref[...])
    else:
        memory = memory_ref[...]
    memory_scr[...] = memory
    stores[0].start()
    memory_b, memory_low = split_two(memory)
    pick = ones_where(touched_t_ref[:, turn : turn + 1] == iota((touch, rows), 1))
    held_b = dot(pick, memory_b)
    held_scr[...] = held_b + dot(pick, memory_low)
    stores[1].start()
    held_b = held_b.astype(BF16)
    gh_scr[...] = dot(held_b, w_hid_ref[...]).astype(BF16)
    stores[2].start()
    live = iota((touch, events), 1) < count_ref[turn]
    member_mask = jnp.logical_and(iota((touch, events), 0) == src_ref[turn : turn + 1, :], live)
    member_f = jnp.where(member_mask, 1.0, 0.0)
    member = member_f.astype(BF16)
    inv = 1.0 / jnp.sum(member_f, axis=1, keepdims=True)
    dst_pick = ones_where(iota((slots, events), 0) == dst_ref[turn : turn + 1, :])
    links_scr[...] = dot_nt(member, dst_pick).astype(BF16)
    stores[3].start()
    angle = freq_ref[...] * gap_ref[turn : turn + 1, :].astype(F32) + phase_ref[...]
    code = jnp.cos(angle).astype(BF16)
    code_mean = (dot_nt(member, code) * inv).astype(BF16)
    base = dot(held_b, w_src_ref[...]) + dot(code_mean, w_code_ref[...])
    base_scr[...] = base.astype(BF16)
    stores[4].start()
    if last:
        static_scr[...] = jnp.zeros_like(static_scr)
        hits_scr[...] = jnp.zeros_like(hits_scr)
    else:
        now = touched_ref[turn : turn + 1, :]
        kept_place = ones_where(iota((rows, touch), 0) == now)
        kept = jnp.where(hit_rows(kept_place), 0.0, memory).astype(BF16)
        wanted = serve_t_ref[:, turn + 1 : turn + 2]
        serve = ones_where(wanted == iota((static_scr.shape[0], rows), 1))
        static_scr[...] = dot(serve, kept).astype(BF16)
        hits_scr[...] = ones_where(wanted == now)
    stores[5].start()
    stores[6].start()
    if turn > 0:

        @pl.when(me_ref[0] == turn - 1)
        def _():
            copy = pltpu.make_async_copy(memory_scr, snap_out, snap_sem)
            copy.start()
            copy.wait()

    for copy in stores:
        copy.wait()


def collect_kernel(
    own_ref,
    links_ref,
    base_ref,
    gh_ref,
    held_ref,
    static_ref,
    hits_ref,
    w_dst_ref,
    w_in_ref,
    total_out,
    count_out,
    links_out,
    base_out,
    gh_out,
    held_out,
    static_out,
    hits_out,
    w_dst_out,
    w_in_out,
    links_scr,
    sems,
):
    half = own_ref.shape[0]
    loads = copies(
        [
            (links_ref.at[:, :half], links_scr),
            (links_ref.at[:, half:], links_out),
            (w_dst_ref, w_dst_out),
            (base_ref, base_out),
            (w_in_ref, w_in_out),
            (gh_ref, gh_out),
            (held_ref, held_out),
            (hits_ref, hits_out),
            (static_ref, static_out),
        ],
        sems,
    )
    for copy in loads:
        copy.start()
    loads[0].wait()
    links = links_scr[...]
    total_out[...] = dot(links, own_ref[...])
    count_own = dot(links, jnp.ones((half, 128), BF16))
    loads[1].wait()
    count_out[...] = count_own + dot(links_out[...], jnp.ones((half, 128), BF16))
    for copy in loads[2:]:
        copy.wait()


def updated(other, total, count, links, base, gh, held, w_dst, w_in):
    raw = total + dot(links, other)
    inv = 1.0 / count
    raw = (raw * jnp.concatenate([inv, inv], axis=1)).astype(BF16)
    aggregate = (dot(raw, w_dst) + base.astype(F32)).astype(BF16)
    gi = dot(aggregate, w_in)
    gh = gh.astype(F32)
    reset_gate = jax.nn.sigmoid(gi[:, :DM] + gh[:, :DM])
    update_gate = jax.nn.sigmoid(gi[:, DM : 2 * DM] + gh[:, DM : 2 * DM])
    candidate = jnp.tanh(gi[:, 2 * DM :] + reset_gate * gh[:, 2 * DM :])
    return (1.0 - update_gate) * candidate + update_gate * held


def update_kernel(
    turn,
    me_ref,
    own_ref,
    other_ref,
    total_ref,
    count_ref,
    links_ref,
    base_ref,
    gh_ref,
    held_ref,
    static_ref,
    hits_ref,
    w_dst_ref,
    w_in_ref,
    *rest,
):
    fresh_out, served_out, kept_out, fresh_kept_out, fresh_scr, served_scr, sems, kept_sems = rest[-8:]
    half = own_ref.shape[0]
    mine = me_ref[0] == turn
    keeps = copies(
        [
            (own_ref, kept_out.at[:half]),
            (other_ref, kept_out.at[half:]),
            (fresh_scr, fresh_kept_out),
        ],
        kept_sems,
    )

    @pl.when(mine)
    def _():
        for copy in keeps[:2]:
            copy.start()

    fresh = updated(
        other_ref[...],
        total_ref[...],
        count_ref[...],
        links_ref[...],
        base_ref[...],
        gh_ref[...],
        held_ref[...],
        w_dst_ref[...],
        w_in_ref[...],
    )
    fresh_scr[...] = fresh
    store = pltpu.make_async_copy(fresh_scr, fresh_out, sems.at[0])
    store.start()

    @pl.when(mine)
    def _():
        keeps[2].start()

    fresh_b = fresh.astype(BF16)
    sends = []
    block = half // 2
    for i in range(2):
        at = slice(i * block, (i + 1) * block)
        served = dot(hits_ref[at, :], fresh_b) + static_ref[at, :].astype(F32)
        served_scr[at, :] = served.astype(BF16)
        copy = pltpu.make_async_copy(served_scr.at[at], served_out.at[at], sems.at[1 + i])
        copy.start()
        sends.append(copy)
    for copy in [store] + sends:
        copy.wait()

    @pl.when(mine)
    def _():
        for copy in keeps:
            copy.wait()


def embedded(live_count, nbr, kept, codes, src_t, fresh_b, w_nbr, w_nbr_code, w_out):
    events = src_t.shape[0]
    near = dot(nbr, kept)
    hidden = dot(near.astype(BF16), w_nbr) + dot(codes, w_nbr_code)
    hidden = jnp.maximum(hidden, 0.0).astype(BF16)
    src_pick = ones_where(src_t == iota((events, fresh_b.shape[0]), 1))
    src_new = dot(src_pick, fresh_b).astype(BF16)
    out = dot(src_new, w_out[:DM, :]) + dot(hidden, w_out[DM:, :])
    live = iota((events, 1), 0) < live_count
    return jnp.where(live, out, 0.0).astype(BF16)


def last_kernel(
    turn,
    me_ref,
    counts_ref,
    own_ref,
    other_ref,
    total_ref,
    count_ref,
    links_ref,
    base_ref,
    gh_ref,
    held_ref,
    static_ref,
    hits_ref,
    w_dst_ref,
    w_in_ref,
    touched_ref,
    nbr_ref,
    codes_ref,
    src_t_ref,
    w_nbr_ref,
    w_nbr_code_ref,
    w_out_ref,
    memory_ref,
    emb_in_ref,
    snap_in_ref,
    emb_out,
    snap_out,
    nbr_scr,
    codes_scr,
    src_t_scr,
    w_nbr_scr,
    w_nbr_code_scr,
    w_out_scr,
    memory_scr,
    snap_scr,
    emb_scr,
    sems,
    out_sems,
):
    @pl.when(me_ref[0] == turn)
    def _():
        loads = copies(
            [
                (memory_ref, memory_scr),
                (nbr_ref, nbr_scr),
                (w_nbr_ref, w_nbr_scr),
                (codes_ref, codes_scr),
                (w_nbr_code_ref, w_nbr_code_scr),
                (src_t_ref, src_t_scr),
                (w_out_ref, w_out_scr),
            ],
            sems,
        )
        for copy in loads:
            copy.start()
        fresh = updated(
            other_ref[...],
            total_ref[...],
            count_ref[...],
            links_ref[...],
            base_ref[...],
            gh_ref[...],
            held_ref[...],
            w_dst_ref[...],
            w_in_ref[...],
        )
        rows, touch = memory_scr.shape[0], touched_ref.shape[1]
        place = ones_where(iota((rows, touch), 0) == touched_ref[turn : turn + 1, :])
        high, low = split_two(fresh)
        for copy in loads:
            copy.wait()
        placed = dot(place, high) + dot(place, low)
        snap_scr[...] = jnp.where(hit_rows(place), placed, memory_scr[...])
        store_snap = pltpu.make_async_copy(snap_scr, snap_out, out_sems.at[0])
        store_snap.start()
        kept = jnp.concatenate([own_ref[...], other_ref[...]], axis=0)
        emb_scr[...] = embedded(
            counts_ref[turn],
            nbr_scr[...],
            kept,
            codes_scr[...].astype(BF16),
            src_t_scr[...],
            high,
            w_nbr_scr[...],
            w_nbr_code_scr[...],
            w_out_scr[...],
        )
        store_emb = pltpu.make_async_copy(emb_scr, emb_out, out_sems.at[1])
        store_emb.start()
        store_snap.wait()
        store_emb.wait()


def neighbours_kernel(after_ref, nbr_ref, out_ref):
    events, slots = out_ref.shape
    block = 64

    def step(i, carry):
        at = pl.ds(pl.multiple_of(i * block, block), block)
        picks = nbr_ref[at, :]
        lanes = iota((block, slots), 1)
        total = jnp.zeros((block, slots), F32)
        for q in range(nbr_ref.shape[1]):
            total += jnp.where(picks[:, q : q + 1] == lanes, 1.0, 0.0)
        out_ref[at, :] = total.astype(BF16)
        return carry

    lax.fori_loop(0, events // block, step, 0)


def codes_kernel(begin, end, after_ref, gap_ref, freq_ref, phase_ref, sum_ref, out_ref):
    block = 64

    def step(i, carry):
        at = pl.ds(pl.multiple_of(i * block, block), block)
        gaps = gap_ref[at, :].astype(F32)
        total = sum_ref[at, :]
        for q in range(begin, end):
            total += jnp.cos(gaps[:, q : q + 1] * freq_ref[...] + phase_ref[...])
        out_ref[at, :] = total
        return carry

    lax.fori_loop(0, gap_ref.shape[0] // block, step, 0)


def tie_kernel(*refs):
    pass


def embed_kernel(
    turns,
    me_ref,
    fresh_ref,
    kept_ref,
    nbr_ref,
    codes_ref,
    src_t_ref,
    count_ref,
    w_nbr_ref,
    w_nbr_code_ref,
    w_out_ref,
    emb_out,
    fresh_scr,
    kept_scr,
    nbr_scr,
    codes_scr,
    emb_scr,
    sems,
    sem,
):
    @pl.when(me_ref[0] < turns - 1)
    def _():
        loads = copies(
            [
                (kept_ref, kept_scr),
                (nbr_ref, nbr_scr),
                (fresh_ref, fresh_scr),
                (codes_ref, codes_scr),
            ],
            sems,
        )
        for copy in loads:
            copy.start()
        for copy in loads:
            copy.wait()
        emb_scr[...] = embedded(
            count_ref[me_ref[0]],
            nbr_scr[...],
            kept_scr[...],
            codes_scr[...].astype(BF16),
            src_t_ref[...],
            fresh_scr[...].astype(BF16),
            w_nbr_ref[...],
            w_nbr_code_ref[...],
            w_out_ref[...],
        )
        copy = pltpu.make_async_copy(emb_scr, emb_out, sem)
        copy.start()
        copy.wait()


def in_hbm(dims, dtype):
    return pltpu.HBM(dims, dtype)


def stay(arrays):
    return [pltpu.with_memory_space_constraint(x, pltpu.HBM) for x in arrays]


def shape(dims, dtype):
    return jax.ShapeDtypeStruct(dims, dtype)


def params(mib=16):
    return pltpu.CompilerParams(vmem_limit_bytes=mib * 1024 * 1024)


def cost(flops, bytes_accessed):
    return pl.CostEstimate(flops=flops, bytes_accessed=bytes_accessed, transcendentals=0)


def body(
    memory,
    touched,
    src_slot,
    ev_count,
    serve_rows,
    dst_slot,
    nbr_slot,
    ev_gap,
    nbr_gap,
    time_freq,
    time_phase,
    w_msg,
    w_in,
    w_hid,
    w_nbr,
    w_out,
):
    me = lax.axis_index("tm")
    core = me % 2
    sections = lax.axis_size("tm")
    shards = lax.axis_size("node")
    rows = memory.shape[0]
    events = src_slot.shape[2]
    slots = serve_rows.shape[2]
    half = slots // 2
    capacity = slots // shards
    part = capacity // 2
    touched = touched[:, 0, :]
    touch = touched.shape[1]

    lists = [
        serve_rows.reshape(-1, 128),
        dst_slot.reshape(-1, 128),
        src_slot.reshape(-1, 128),
        ev_gap.reshape(-1, 128),
    ]
    lines = sum(x.shape[0] for x in lists) + 4
    packed = pl.pallas_call(
        pack_kernel,
        out_shape=shape((sections, lines, 128), jnp.int32),
        in_specs=[HBM] * 4 + [SMEM],
        out_specs=HBM,
        scratch_shapes=[
            pltpu.VMEM((lines, 128), jnp.int32),
            pltpu.SemaphoreType.DMA((4,)),
            pltpu.SemaphoreType.DMA((sections,)),
        ],
        compiler_params=params(),
        name="pack",
    )(*stay(lists), ev_count)
    everyone = lax.all_to_all(packed, "tm", split_axis=0, concat_axis=0, tiled=True).reshape(
        sections, -1
    )
    serve_all = everyone[:, :slots].reshape(sections, shards, 2, part)
    serve_own = jnp.where(core == 0, serve_all[:, :, 0], serve_all[:, :, 1])
    serve_t = serve_own.reshape(sections, half).T
    at = slots
    dst_all = everyone[:, at : at + events]
    at += events
    src_all = everyone[:, at : at + events]
    at += events
    gap_all = everyone[:, at : at + events]
    at += events
    count_all = everyone[:, at]

    def reordered(slot):
        place = slot % capacity
        mine = (place // part) == core
        return (slot // capacity) * part + place % part + jnp.where(mine, 0, half)

    dst_all = reordered(dst_all)
    touched_t = touched.T
    me_s = me.reshape(1).astype(jnp.int32)
    freq = jnp.pad(time_freq, (0, CODE - TD)).reshape(CODE, 1)
    phase = jnp.pad(time_phase, (0, CODE - TD)).reshape(CODE, 1)
    w_src, w_dst, w_code = w_msg[:DM], w_msg[DM : 2 * DM], w_msg[2 * DM :]
    w_code = jnp.pad(w_code, ((0, CODE - TD), (0, 0)))
    w_nbr_code = jnp.pad(w_nbr[DM:], ((0, CODE - TD), (0, 0)))
    w_nbr_row = w_nbr[:DM]

    served = pl.pallas_call(
        first_serve_kernel,
        out_shape=shape((half, DM), BF16),
        in_specs=[VMEM] * 2,
        out_specs=VMEM,
        compiler_params=params(),
        name="first_serve",
    )(serve_t, memory)

    nbr_t = reordered(nbr_slot[0, 0]).T
    nbr_gap_t = nbr_gap[0, 0].T
    freq_row, phase_row = freq.reshape(1, CODE), phase.reshape(1, CODE)

    def count_neighbours(after):
        return pl.pallas_call(
            neighbours_kernel,
            out_shape=in_hbm((events, slots), BF16),
            in_specs=[HBM, VMEM],
            out_specs=VMEM,
            compiler_params=params(),
            cost_estimate=cost(10**9, 2**20),
            name="neighbour_counts",
        )(*stay([after]), nbr_t)

    def code_sums(begin, end, after, total):
        return pl.pallas_call(
            functools.partial(codes_kernel, begin, end),
            out_shape=in_hbm((events, CODE), F32),
            in_specs=[HBM] + [VMEM] * 4,
            out_specs=VMEM,
            compiler_params=params(),
            cost_estimate=cost(10**9, 2**20),
            name="codes",
        )(*stay([after]), nbr_gap_t, freq_row, phase_row, total)

    src_t = src_slot.reshape(events, 1)
    memory_now = memory
    fresh = memory
    nbr_codes = jnp.zeros((events, CODE), F32)
    swap = [(i, i ^ 1) for i in range(sections)]
    whole = (
        in_hbm((rows, DM), F32),
        in_hbm((touch, DM), F32),
        in_hbm((touch, 3 * DM), BF16),
        in_hbm((touch, slots), BF16),
        in_hbm((touch, DM), BF16),
        in_hbm((half, DM), BF16),
        in_hbm((half, touch), BF16),
    )
    first_outs = (
        in_hbm((touch, DM), F32),
        in_hbm((half, DM), BF16),
        in_hbm((slots, DM), BF16),
        in_hbm((touch, DM), F32),
    )
    snap, keeps = (), ()
    code_steps = {1: (0, 4), 2: (4, 7), 3: (7, nbr_slot.shape[2])}
    for turn in range(sections):
        last = turn + 1 == sections
        own = lax.all_to_all(
            served.reshape(shards, part, DM), "node", split_axis=0, concat_axis=0, tiled=True
        ).reshape(half, DM)
        prepared = pl.pallas_call(
            functools.partial(prepare_kernel, turn, last),
            out_shape=whole + (in_hbm((rows, DM), F32),) * (turn > 0),
            in_specs=[SMEM] + [VMEM] * 7 + [SMEM] + [VMEM] * 6 + [HBM] * len(snap),
            out_specs=(HBM,) * (7 + (turn > 0)),
            scratch_shapes=[pltpu.VMEM(x.shape, x.dtype) for x in whole]
            + [pltpu.SemaphoreType.DMA((len(whole),)), pltpu.SemaphoreType.DMA],
            input_output_aliases={15: 7} if snap else {},
            compiler_params=params(),
            cost_estimate=cost(2 * 10**9, 2**22),
            name="prepare",
        )(
            me_s,
            memory_now,
            fresh,
            touched,
            touched_t,
            src_all,
            dst_all,
            gap_all,
            count_all,
            serve_t,
            freq,
            phase,
            w_src,
            w_code,
            w_hid,
            *stay(snap),
        )
        memory_now, held, gh, links, base, static, hits = prepared[:7]
        snap = prepared[7:]
        waits = [base]
        if turn in code_steps:
            nbr_codes = code_sums(*code_steps[turn], fresh, nbr_codes)
            waits.append(nbr_codes)
        if turn == 4:
            nbr_counts = count_neighbours(fresh)
            waits.append(nbr_counts)
        if last:
            emb = embed(
                sections,
                me_s,
                keeps[1],
                keeps[0],
                (nbr_counts, nbr_codes, src_t, count_all, w_nbr_row, w_nbr_code, w_out),
            )
            waits.append(emb)
        own = pl.pallas_call(
            tie_kernel,
            out_shape=shape(own.shape, own.dtype),
            in_specs=[ANY] + [HBM] * len(waits),
            out_specs=ANY,
            input_output_aliases={0: 0},
            compiler_params=params(1),
            name="tie",
        )(own, *stay(waits))
        other = lax.ppermute(own, "tm", swap)
        stored = (links, base, gh, held, static, hits, w_dst, w_in)
        ready = pl.pallas_call(
            collect_kernel,
            out_shape=(
                shape((touch, DM), F32),
                shape((touch, 128), F32),
                shape((touch, half), BF16),
            )
            + tuple(shape(x.shape, x.dtype) for x in stored[1:]),
            in_specs=[VMEM] + [HBM] * 8,
            out_specs=(VMEM,) * 10,
            scratch_shapes=[pltpu.VMEM((touch, half), BF16), pltpu.SemaphoreType.DMA((9,))],
            compiler_params=params(),
            cost_estimate=cost(10**9, 2**22),
            name="collect",
        )(own, *stay(stored))
        if last:
            break
        fresh, served, *keeps = pl.pallas_call(
            functools.partial(update_kernel, turn),
            out_shape=first_outs,
            in_specs=[SMEM] + [VMEM] * 12 + [HBM] * len(keeps),
            out_specs=(HBM,) * 4,
            scratch_shapes=[
                pltpu.VMEM((touch, DM), F32),
                pltpu.VMEM((half, DM), BF16),
                pltpu.SemaphoreType.DMA((3,)),
                pltpu.SemaphoreType.DMA((3,)),
            ],
            input_output_aliases={13: 2, 14: 3} if keeps else {},
            compiler_params=params(),
            cost_estimate=cost(10**9, 2**22),
            name="update",
        )(me_s, own, other, *ready, *stay(keeps))
    late = (nbr_counts, nbr_codes, src_t, w_nbr_row, w_nbr_code, w_out, memory_now, emb, snap[0])
    emb, snap = pl.pallas_call(
        functools.partial(last_kernel, turn),
        out_shape=(in_hbm((events, DM), BF16), in_hbm((rows, DM), F32)),
        in_specs=[SMEM] * 2 + [VMEM] * 13 + [HBM] * 9,
        out_specs=(HBM,) * 2,
        scratch_shapes=[
            pltpu.VMEM((events, slots), BF16),
            pltpu.VMEM((events, CODE), F32),
            pltpu.VMEM((events, 1), jnp.int32),
            pltpu.VMEM((DM, DM), BF16),
            pltpu.VMEM((CODE, DM), BF16),
            pltpu.VMEM((2 * DM, DM), BF16),
            pltpu.VMEM((rows, DM), F32),
            pltpu.VMEM((rows, DM), F32),
            pltpu.VMEM((events, DM), BF16),
            pltpu.SemaphoreType.DMA((7,)),
            pltpu.SemaphoreType.DMA((2,)),
        ],
        input_output_aliases={22: 0, 23: 1},
        compiler_params=params(),
        name="last",
    )(me_s, count_all, own, other, *ready, touched, *stay(late))
    return (emb[None, None], snap[None])


def embed(turns, me_s, fresh, kept, rest):
    nbr_counts, nbr_codes, *small = rest
    events = nbr_counts.shape[0]
    return pl.pallas_call(
        functools.partial(embed_kernel, turns),
        out_shape=in_hbm((events, DM), BF16),
        in_specs=[SMEM] + [HBM] * 4 + [VMEM] + [SMEM] + [VMEM] * 3,
        out_specs=HBM,
        scratch_shapes=[
            pltpu.VMEM(fresh.shape, F32),
            pltpu.VMEM(kept.shape, BF16),
            pltpu.VMEM(nbr_counts.shape, BF16),
            pltpu.VMEM(nbr_codes.shape, F32),
            pltpu.VMEM((events, DM), BF16),
            pltpu.SemaphoreType.DMA((4,)),
            pltpu.SemaphoreType.DMA,
        ],
        compiler_params=params(),
        cost_estimate=cost(10**9, 2**22),
        name="embed",
    )(me_s, *stay([fresh, kept, nbr_counts, nbr_codes]), *small)


def solution(mesh):
    return jax.shard_map(
        body,
        mesh=mesh,
        in_specs=(
            P("node", None),
            P(None, "node", None),
            P("tm", "node", None),
            P("tm", "node"),
            P("tm", "node", None),
            P("tm", "node", None),
            P("tm", "node", None, None),
            P("tm", "node", None),
            P("tm", "node", None, None),
            P(),
            P(),
            P(),
            P(),
            P(),
            P(),
            P(),
        ),
        out_specs=(P("tm", "node", None, None), P("tm", "node", None)),
        check_vma=False,
    )
```

```python
import functools

import jax
import jax.numpy as jnp
from jax import lax
from jax.experimental import pallas as pl
from jax.experimental.pallas import tpu as pltpu
from jax.sharding import PartitionSpec as P

DM = 256
TD = 100
CODE = 128
GAPS = 1024
NBRS = 10
F32 = jnp.float32
BF16 = jnp.bfloat16
VMEM = pl.BlockSpec(memory_space=pltpu.VMEM)
SMEM = pl.BlockSpec(memory_space=pltpu.SMEM)
ANY = pl.BlockSpec(memory_space=pl.ANY)
HBM = pl.BlockSpec(memory_space=pltpu.HBM)


def dot(a, b):
    return jnp.dot(a, b, preferred_element_type=F32)


def dot_nt(a, b):
    return lax.dot_general(a, b, (((1,), (1,)), ((), ())), preferred_element_type=F32)


def iota(shape, axis):
    return lax.broadcasted_iota(jnp.int32, shape, axis)


def ones_where(mask):
    return jnp.where(mask, 1.0, 0.0).astype(BF16)


def same16(a, b):
    mask = a.astype(jnp.int16) == b.astype(jnp.int16)
    return jnp.where(mask, jnp.ones((), BF16), jnp.zeros((), BF16))


def pick_rows(height, row):
    row = row.astype(jnp.int16)
    base = iota((16, row.shape[1]), 0).astype(jnp.int16)
    one, zero = jnp.ones((), BF16), jnp.zeros((), BF16)
    return jnp.concatenate(
        [jnp.where(base + jnp.int16(i) == row, one, zero) for i in range(0, height, 16)], axis=0
    )


def split_two(x):
    high = x.astype(BF16)
    return high, (x - high.astype(F32)).astype(BF16)


def hit_rows(place):
    return jnp.max(place.astype(F32), axis=1, keepdims=True) > 0.5


def copies(pairs, sems):
    return [pltpu.make_async_copy(src, dst, sems.at[i]) for i, (src, dst) in enumerate(pairs)]


def pack_kernel(serve_ref, dst_ref, src_ref, gap_ref, count_ref, out_ref, scr, in_sems, out_sems):
    at, pairs = 0, []
    for ref in (serve_ref, dst_ref, src_ref, gap_ref):
        pairs.append((ref, scr.at[at : at + ref.shape[0]]))
        at += ref.shape[0]
    loads = copies(pairs, in_sems)
    for copy in loads:
        copy.start()
    scr[at:, :] = jnp.full((scr.shape[0] - at, 128), count_ref[0, 0], jnp.int32)
    for copy in loads:
        copy.wait()
    sends = copies([(scr, out_ref.at[i]) for i in range(out_ref.shape[0])], out_sems)
    for copy in sends:
        copy.start()
    for copy in sends:
        copy.wait()


def first_serve_kernel(serve_ref, memory_ref, *rest):
    served_out, memory_out = rest[-2:]
    memory = memory_ref[...].astype(BF16)
    memory_out[...] = memory
    pick = same16(serve_ref[:, 0:1], iota((serve_ref.shape[0], memory.shape[0]), 1))
    served_out[...] = dot(pick, memory).astype(BF16)


def table_kernel(freq_ref, phase_ref, high_out, low_out):
    gap = iota(high_out.shape, 0).astype(F32)
    high, low = split_two(jnp.cos(gap * freq_ref[...] + phase_ref[...]))
    high_out[...] = high
    low_out[...] = low


def links_kernel(src_ref, dst_ref, gap_ref, count_ref, table_ref, w_code_ref, links_out, code_out, inv_out):
    turn = pl.program_id(0)
    touch, slots = links_out.shape[1:]
    events = src_ref.shape[1]
    row = pl.ds(turn, 1)
    live = iota((touch, events), 1) < count_ref[turn]
    member_mask = jnp.logical_and(iota((touch, events), 0) == src_ref[row, :], live)
    member_f = jnp.where(member_mask, 1.0, 0.0)
    member = member_f.astype(BF16)
    inv = 1.0 / jnp.sum(member_f, axis=1, keepdims=True)
    inv_out[0] = jnp.broadcast_to(inv, inv_out.shape[1:])
    dst_pick = pick_rows(slots, dst_ref[row, :])
    links_out[0] = dot_nt(member, dst_pick).astype(BF16)
    gap_pick = pick_rows(table_ref.shape[0], gap_ref[row, :])
    gap_count = dot_nt(member, gap_pick).astype(BF16)
    code_mean = (dot(gap_count, table_ref[...]) * inv).astype(BF16)
    code_out[0] = dot(code_mean, w_code_ref[2 * DM :, :]).astype(BF16)


def ready_kernel(
    turn,
    last,
    me_ref,
    own_ref,
    kept_ref,
    fresh_ref,
    touched_ref,
    touched_t_ref,
    serve_t_ref,
    w_msg_ref,
    w_hid_ref,
    links_ref,
    code_ref,
    inv_ref,
    *rest,
):
    outs = rest[turn > 1 : (turn > 1) + 9]
    total_out, inv_out, links_out, base_out, gh_out, held_out, static_out, hits_out, kept_out = outs
    links_scr, code_scr, memory_scr, sems, snap_sem = rest[-5:]
    rows, touch, half = kept_ref.shape[0], touched_ref.shape[1], own_ref.shape[0]
    loads = copies(
        [
            (links_ref.at[turn, :, :half], links_scr),
            (links_ref.at[turn, :, half:], links_out),
            (code_ref.at[turn], code_scr),
            (inv_ref.at[turn], inv_out),
        ],
        sems,
    )
    for copy in loads:
        copy.start()
    memory = kept_ref[...]
    if turn > 0:
        place = pick_rows(rows, touched_ref[turn - 1 : turn, :])
        memory = memory + dot(place, fresh_ref[...]).astype(BF16)
        snap_store = pltpu.make_async_copy(memory_scr, rest[-6], snap_sem)

        @pl.when(me_ref[0] == turn - 1)
        def _():
            memory_scr[...] = memory.astype(F32)
            snap_store.start()

    pick = same16(touched_t_ref[:, turn : turn + 1], iota((touch, rows), 1))
    held = dot(pick, memory).astype(BF16)
    held_out[...] = held
    gh_out[...] = dot(held, w_hid_ref[...])
    base = dot(held, w_msg_ref[:DM, :])
    now = touched_ref[turn : turn + 1, :]
    hit = dot(pick_rows(rows, now), jnp.ones((touch, 128), BF16))
    free = (1.0 - hit).astype(BF16)
    kept = memory * jnp.concatenate([free, free], axis=1)
    kept_out[...] = kept
    if not last:
        wanted = serve_t_ref[:, turn + 1 : turn + 2]
        serve = same16(wanted, iota((half, rows), 1))
        static_out[...] = dot(serve, kept).astype(BF16)
        hits_out[...] = same16(wanted, now)
    loads[0].wait()
    total_out[...] = dot(links_scr[...], own_ref[...])
    loads[2].wait()
    base_out[...] = base + code_scr[...].astype(F32)
    loads[1].wait()
    loads[3].wait()
    if turn > 0:

        @pl.when(me_ref[0] == turn - 1)
        def _():
            snap_store.wait()


def updated(other, total, inv, links, base, gh, held, w_dst, w_in):
    raw = total + dot(links, other)
    raw = (raw * jnp.concatenate([inv, inv], axis=1)).astype(BF16)
    aggregate = (dot(raw, w_dst) + base).astype(BF16)
    gi = dot(aggregate, w_in)
    reset_gate = jax.nn.sigmoid(gi[:, :DM] + gh[:, :DM])
    update_gate = jax.nn.sigmoid(gi[:, DM : 2 * DM] + gh[:, DM : 2 * DM])
    candidate = jnp.tanh(gi[:, 2 * DM :] + reset_gate * gh[:, 2 * DM :])
    return (1.0 - update_gate) * candidate + update_gate * held.astype(F32)


def update_kernel(
    turn,
    me_ref,
    own_ref,
    other_ref,
    total_ref,
    inv_ref,
    links_ref,
    base_ref,
    gh_ref,
    held_ref,
    static_ref,
    hits_ref,
    w_msg_ref,
    w_in_ref,
    *rest,
):
    fresh_out, served_out, kept_out, fresh_kept_out, kept_sems = rest[-5:]
    half = own_ref.shape[0]
    mine = me_ref[0] == turn
    keeps = copies(
        [
            (own_ref, kept_out.at[:half]),
            (other_ref, kept_out.at[half:]),
            (fresh_out, fresh_kept_out),
        ],
        kept_sems,
    )

    @pl.when(mine)
    def _():
        for copy in keeps[:2]:
            copy.start()

    fresh = updated(
        other_ref[...],
        total_ref[...],
        inv_ref[...],
        links_ref[...],
        base_ref[...],
        gh_ref[...],
        held_ref[...],
        w_msg_ref[DM : 2 * DM, :],
        w_in_ref[...],
    )
    fresh_b = fresh.astype(BF16)
    fresh_out[...] = fresh_b

    @pl.when(mine)
    def _():
        keeps[2].start()

    served = dot(hits_ref[...], fresh_b) + static_ref[...].astype(F32)
    served_out[...] = served.astype(BF16)

    @pl.when(mine)
    def _():
        for copy in keeps:
            copy.wait()


def embedded(live_count, nbr, kept, codes, src_t, fresh_b, w_nbr, w_nbr_code, w_out):
    events = src_t.shape[0]
    near = dot(nbr, kept)
    hidden = dot(near.astype(BF16), w_nbr) + dot(codes, w_nbr_code)
    hidden = jnp.maximum(hidden, 0.0).astype(BF16)
    src_pick = same16(src_t, iota((events, fresh_b.shape[0]), 1))
    src_new = dot(src_pick, fresh_b).astype(BF16)
    out = dot(src_new, w_out[:DM, :]) + dot(hidden, w_out[DM:, :])
    live = iota((events, 1), 0) < live_count
    return jnp.where(live, out, 0.0).astype(BF16)


def last_kernel(
    turn,
    me_ref,
    counts_ref,
    own_ref,
    other_ref,
    total_ref,
    inv_ref,
    links_ref,
    base_ref,
    gh_ref,
    held_ref,
    memory_ref,
    w_msg_ref,
    w_in_ref,
    touched_ref,
    nbr_ref,
    codes_ref,
    lists_ref,
    w_nbr_ref,
    w_out_ref,
    rows_ref,
    fresh_kept_ref,
    snap_in_ref,
    emb_out,
    snap_out,
    rows_scr,
    fresh_scr,
    snap_scr,
    emb_scr,
    rows_sems,
    out_sems,
):
    mine = me_ref[0] == turn
    half = own_ref.shape[0]
    early = copies([(rows_ref, rows_scr), (fresh_kept_ref, fresh_scr)], rows_sems)
    snap_store = pltpu.make_async_copy(snap_scr, snap_out, out_sems.at[0])

    @pl.when(jnp.logical_not(mine))
    def _():
        for copy in early:
            copy.start()
        for copy in early:
            copy.wait()

    @pl.when(mine)
    def _():
        rows_scr[:half, :] = own_ref[...]
        rows_scr[half:, :] = other_ref[...]
        fresh = updated(
            other_ref[...],
            total_ref[...],
            inv_ref[...],
            links_ref[...],
            base_ref[...],
            gh_ref[...],
            held_ref[...],
            w_msg_ref[DM : 2 * DM, :],
            w_in_ref[...],
        )
        fresh_scr[...] = fresh.astype(BF16)
        rows, touch = memory_ref.shape[0], touched_ref.shape[1]
        place = pick_rows(rows, touched_ref[turn : turn + 1, :])
        high, low = split_two(fresh)
        snap_scr[...] = memory_ref[...].astype(F32) + (dot(place, high) + dot(place, low))
        snap_store.start()

    emb_scr[...] = embedded(
        counts_ref[me_ref[0]],
        nbr_ref[...],
        rows_scr[...],
        codes_ref[...],
        lists_ref[:, 2 * NBRS : 2 * NBRS + 1],
        fresh_scr[...],
        w_nbr_ref[:DM, :],
        w_nbr_ref[DM:, :],
        w_out_ref,
    )
    store_emb = pltpu.make_async_copy(emb_scr, emb_out, out_sems.at[1])
    store_emb.start()

    @pl.when(mine)
    def _():
        snap_store.wait()

    store_emb.wait()


def count_block(lists, number, begin, width):
    lanes = iota((lists.shape[0], width), 1)
    total = same16(lists[:, begin : begin + 1], lanes)
    for q in range(begin + 1, begin + number):
        total += same16(lists[:, q : q + 1], lanes)
    return total


def neighbours_kernel(after_ref, lists_ref, out_ref):
    block = 64

    def step(i, carry):
        at = pl.ds(pl.multiple_of(i * block, block), block)
        out_ref[at, :] = count_block(lists_ref[at, :], NBRS, 0, out_ref.shape[1])
        return carry

    lax.fori_loop(0, out_ref.shape[0] // block, step, 0)


def codes_kernel(after_ref, lists_ref, high_ref, low_ref, out_ref):
    block = 128

    def step(i, carry):
        at = pl.ds(pl.multiple_of(i * block, block), block)
        counts = count_block(lists_ref[at, :], NBRS, NBRS, high_ref.shape[0])
        out_ref[at, :] = (dot(counts, high_ref[...]) + dot(counts, low_ref[...])).astype(BF16)
        return carry

    lax.fori_loop(0, out_ref.shape[0] // block, step, 0)


def tie_kernel(*refs):
    pass


def in_hbm(dims, dtype):
    return pltpu.HBM(dims, dtype)


def stay(arrays):
    return [pltpu.with_memory_space_constraint(x, pltpu.HBM) for x in arrays]


def shape(dims, dtype):
    return jax.ShapeDtypeStruct(dims, dtype)


def params(mib=16):
    return pltpu.CompilerParams(vmem_limit_bytes=mib * 1024 * 1024)


def cost(flops, bytes_accessed):
    return pl.CostEstimate(flops=flops, bytes_accessed=bytes_accessed, transcendentals=0)


def body(
    memory,
    touched,
    src_slot,
    ev_count,
    serve_rows,
    dst_slot,
    nbr_slot,
    ev_gap,
    nbr_gap,
    time_freq,
    time_phase,
    w_msg,
    w_in,
    w_hid,
    w_nbr,
    w_out,
):
    me = lax.axis_index("tm")
    core = me % 2
    sections = lax.axis_size("tm")
    shards = lax.axis_size("node")
    rows = memory.shape[0]
    events = src_slot.shape[2]
    slots = serve_rows.shape[2]
    half = slots // 2
    capacity = slots // shards
    part = capacity // 2
    touched = touched[:, 0, :]
    touch = touched.shape[1]

    lists = [
        serve_rows.reshape(-1, 128),
        dst_slot.reshape(-1, 128),
        src_slot.reshape(-1, 128),
        ev_gap.reshape(-1, 128),
    ]
    lines = sum(x.shape[0] for x in lists) + 4
    packed = pl.pallas_call(
        pack_kernel,
        out_shape=shape((sections, lines, 128), jnp.int32),
        in_specs=[HBM] * 4 + [SMEM],
        out_specs=HBM,
        scratch_shapes=[
            pltpu.VMEM((lines, 128), jnp.int32),
            pltpu.SemaphoreType.DMA((4,)),
            pltpu.SemaphoreType.DMA((sections,)),
        ],
        compiler_params=params(),
        name="pack",
    )(*stay(lists), ev_count)
    everyone = lax.all_to_all(packed, "tm", split_axis=0, concat_axis=0, tiled=True).reshape(
        sections, -1
    )
    serve_all = everyone[:, :slots].reshape(sections, shards, 2, part)
    serve_own = jnp.where(core == 0, serve_all[:, :, 0], serve_all[:, :, 1])
    serve_t = serve_own.reshape(sections, half).T
    at = slots
    dst_all = everyone[:, at : at + events]
    at += events
    src_all = everyone[:, at : at + events]
    at += events
    gap_all = everyone[:, at : at + events]
    at += events
    count_all = everyone[:, at]

    def reordered(slot):
        place = slot % capacity
        mine = (place // part) == core
        return (slot // capacity) * part + place % part + jnp.where(mine, 0, half)

    dst_all = reordered(dst_all)
    touched_t = touched.T
    me_s = me.reshape(1).astype(jnp.int32)
    freq = jnp.pad(time_freq, (0, CODE - TD)).reshape(1, CODE)
    phase = jnp.pad(time_phase, (0, CODE - TD)).reshape(1, CODE)
    w_msg = jnp.pad(w_msg, ((0, CODE - TD), (0, 0)))
    w_nbr = jnp.pad(w_nbr, ((0, CODE - TD), (0, 0)))

    def call(kernel, name, outs, ins, operands, **more):
        return pl.pallas_call(
            kernel,
            out_shape=outs,
            in_specs=ins,
            compiler_params=params(),
            cost_estimate=cost(10**9, 2**22),
            name=name,
            **more,
        )(*operands)

    table, table_low = call(
        table_kernel,
        "table",
        (shape((GAPS, CODE), BF16),) * 2,
        [VMEM] * 2,
        (freq, phase),
        out_specs=(VMEM,) * 2,
    )
    served, memory_now = pl.pallas_call(
        first_serve_kernel,
        out_shape=(shape((half, DM), BF16), shape((rows, DM), BF16)),
        in_specs=[VMEM] * 2 + [ANY] * 4,
        out_specs=(VMEM,) * 2,
        compiler_params=params(),
        name="first_serve",
    )(serve_t, memory, touched, touched_t, table, w_msg)

    links, code, inv = call(
        links_kernel,
        "links",
        (
            in_hbm((sections, touch, slots), BF16),
            in_hbm((sections, touch, DM), BF16),
            in_hbm((sections, touch, 128), F32),
        ),
        [VMEM] * 3 + [SMEM] + [VMEM] * 2,
        (src_all, dst_all, gap_all, count_all, table, w_msg),
        out_specs=(
            pl.BlockSpec((1, touch, slots), lambda t: (t, 0, 0)),
            pl.BlockSpec((1, touch, DM), lambda t: (t, 0, 0)),
            pl.BlockSpec((1, touch, 128), lambda t: (t, 0, 0)),
        ),
        grid=(sections,),
    )
    lists_t = jnp.concatenate(
        [reordered(nbr_slot[0, 0]), nbr_gap[0, 0], src_slot.reshape(1, events)], axis=0
    ).T
    fresh = memory_now
    snap, keeps = (), ()
    swap = [(i, i ^ 1) for i in range(sections)]
    for turn in range(sections):
        last = turn + 1 == sections
        own = lax.all_to_all(
            served.reshape(shards, part, DM), "node", split_axis=0, concat_axis=0, tiled=True
        ).reshape(half, DM)
        if turn == 1:
            nbr_counts = call(
                neighbours_kernel,
                "neighbour_counts",
                in_hbm((events, slots), BF16),
                [HBM, VMEM],
                (*stay([fresh]), lists_t),
                out_specs=VMEM,
            )
            nbr_codes = call(
                codes_kernel,
                "codes",
                in_hbm((events, CODE), BF16),
                [HBM] + [VMEM] * 3,
                (*stay([fresh]), lists_t, table, table_low),
                out_specs=VMEM,
            )
        if turn < 2:
            beside = stay([links] if turn == 0 else [nbr_counts, nbr_codes, w_nbr])
            own = pl.pallas_call(
                tie_kernel,
                out_shape=shape(own.shape, own.dtype),
                in_specs=[ANY] + [HBM] * len(beside),
                out_specs=ANY,
                input_output_aliases={0: 0},
                compiler_params=params(1),
                name="tie",
            )(own, *beside)
        other = lax.ppermute(own, "tm", swap)
        *ready, memory_now = call(
            functools.partial(ready_kernel, turn, last),
            "ready",
            (
                shape((touch, DM), F32),
                shape((touch, 128), F32),
                shape((touch, half), BF16),
                shape((touch, DM), F32),
                shape((touch, 3 * DM), F32),
                shape((touch, DM), BF16),
                shape((half, DM), BF16),
                shape((half, touch), BF16),
                (in_hbm if turn == 0 else shape)((rows, DM), BF16),
            )
            + (in_hbm((rows, DM), F32),) * (turn > 0),
            [SMEM] + [VMEM] * 8 + [HBM] * (3 + len(snap)),
            (
                me_s,
                own,
                memory_now,
                fresh,
                touched,
                touched_t,
                serve_t,
                w_msg,
                w_hid,
                *stay((links, code, inv) + snap),
            ),
            out_specs=(VMEM,) * 9 + (HBM,) * (turn > 0),
            scratch_shapes=[
                pltpu.VMEM((touch, half), BF16),
                pltpu.VMEM((touch, DM), BF16),
                pltpu.VMEM((rows, DM), F32),
                pltpu.SemaphoreType.DMA((4,)),
                pltpu.SemaphoreType.DMA,
            ],
            input_output_aliases={12: 9} if snap else {},
        )
        if turn > 0:
            snap, memory_now = (memory_now,), ready.pop()
        else:
            snap = ()
        if last:
            break
        fresh, served, *keeps = call(
            functools.partial(update_kernel, turn),
            "update",
            (
                (in_hbm if turn == 0 else shape)((touch, DM), BF16),
                shape((half, DM), BF16),
                in_hbm((slots, DM), BF16),
                in_hbm((touch, DM), BF16),
            ),
            [SMEM] + [VMEM] * 12 + [HBM] * len(keeps),
            (me_s, own, other, *ready, w_msg, w_in, *stay(keeps)),
            out_specs=(VMEM,) * 2 + (HBM,) * 2,
            scratch_shapes=[pltpu.SemaphoreType.DMA((3,))],
            input_output_aliases={13: 2, 14: 3} if keeps else {},
        )
    late = (nbr_counts, nbr_codes, lists_t, w_nbr, w_out)
    emb, snap = call(
        functools.partial(last_kernel, turn),
        "last",
        (in_hbm((events, DM), BF16), in_hbm((rows, DM), F32)),
        [SMEM] * 2 + [VMEM] * 17 + [HBM] * 3,
        (
            me_s,
            count_all,
            own,
            other,
            *ready[:6],
            memory_now,
            w_msg,
            w_in,
            touched,
            *late,
            *stay((*keeps, *snap)),
        ),
        out_specs=(HBM,) * 2,
        scratch_shapes=[
            pltpu.VMEM((slots, DM), BF16),
            pltpu.VMEM((touch, DM), BF16),
            pltpu.VMEM((rows, DM), F32),
            pltpu.VMEM((events, DM), BF16),
            pltpu.SemaphoreType.DMA((2,)),
            pltpu.SemaphoreType.DMA((2,)),
        ],
        input_output_aliases={21: 1},
    )
    return (emb[None, None], snap[None])


def solution(mesh):
    return jax.shard_map(
        body,
        mesh=mesh,
        in_specs=(
            P("node", None),
            P(None, "node", None),
            P("tm", "node", None),
            P("tm", "node"),
            P("tm", "node", None),
            P("tm", "node", None),
            P("tm", "node", None, None),
            P("tm", "node", None),
            P("tm", "node", None, None),
            P(),
            P(),
            P(),
            P(),
            P(),
            P(),
            P(),
        ),
        out_specs=(P("tm", "node", None, None), P("tm", "node", None)),
        check_vma=False,
    )
```

```python
import functools

import jax
import jax.numpy as jnp
from jax import lax
from jax.experimental import pallas as pl
from jax.experimental.pallas import tpu as pltpu
from jax.sharding import PartitionSpec as P

DM = 256
TD = 100
CODE = 128
GAPS = 1024
NBRS = 10
FIRST = 5
F32 = jnp.float32
BF16 = jnp.bfloat16
VMEM = pl.BlockSpec(memory_space=pltpu.VMEM)
SMEM = pl.BlockSpec(memory_space=pltpu.SMEM)
ANY = pl.BlockSpec(memory_space=pl.ANY)
HBM = pl.BlockSpec(memory_space=pltpu.HBM)


def dot(a, b):
    return jnp.dot(a, b, preferred_element_type=F32)


def dot_nt(a, b):
    return lax.dot_general(a, b, (((1,), (1,)), ((), ())), preferred_element_type=F32)


def iota(shape, axis):
    return lax.broadcasted_iota(jnp.int32, shape, axis)


def same16(a, b):
    mask = a.astype(jnp.int16) == b.astype(jnp.int16)
    return jnp.where(mask, jnp.ones((), BF16), jnp.zeros((), BF16))


def pick_rows(height, row):
    row = row.astype(jnp.int16)
    base = iota((16, row.shape[1]), 0).astype(jnp.int16)
    one, zero = jnp.ones((), BF16), jnp.zeros((), BF16)
    return jnp.concatenate(
        [jnp.where(base + jnp.int16(i) == row, one, zero) for i in range(0, height, 16)], axis=0
    )


def split_two(x):
    high = x.astype(BF16)
    return high, (x - high.astype(F32)).astype(BF16)


def copies(pairs, sems):
    return [pltpu.make_async_copy(src, dst, sems.at[i]) for i, (src, dst) in enumerate(pairs)]


def pack_kernel(serve_ref, dst_ref, src_ref, gap_ref, count_ref, out_ref, scr, in_sems, out_sems):
    at, pairs = 0, []
    for ref in (serve_ref, dst_ref, src_ref, gap_ref):
        pairs.append((ref, scr.at[at : at + ref.shape[0]]))
        at += ref.shape[0]
    loads = copies(pairs, in_sems)
    for copy in loads:
        copy.start()
    scr[at:, :] = jnp.full((scr.shape[0] - at, 128), count_ref[0, 0], jnp.int32)
    for copy in loads:
        copy.wait()
    sends = copies([(scr, out_ref.at[i]) for i in range(out_ref.shape[0])], out_sems)
    for copy in sends:
        copy.start()
    for copy in sends:
        copy.wait()


def first_serve_kernel(serve_ref, memory_ref, *rest):
    served_out, memory_out = rest[-2:]
    memory = memory_ref[...].astype(BF16)
    memory_out[...] = memory
    pick = same16(serve_ref[:, 0:1], iota((serve_ref.shape[0], memory.shape[0]), 1))
    served_out[...] = dot(pick, memory).astype(BF16)


def table_kernel(freq_ref, phase_ref, high_out, low_out):
    gap = iota(high_out.shape, 0).astype(F32)
    high, low = split_two(jnp.cos(gap * freq_ref[...] + phase_ref[...]))
    high_out[...] = high
    low_out[...] = low


def links_kernel(begin, after_ref, src_ref, dst_ref, gap_ref, count_ref, table_ref, w_code_ref, links_out, code_out, inv_out):
    turn = begin + pl.program_id(0)
    touch, slots = links_out.shape[1:]
    events = src_ref.shape[1]
    row = pl.ds(turn, 1)
    live = iota((touch, events), 1) < count_ref[turn]
    member_mask = jnp.logical_and(iota((touch, events), 0) == src_ref[row, :], live)
    member_f = jnp.where(member_mask, 1.0, 0.0)
    member = member_f.astype(BF16)
    inv = 1.0 / jnp.sum(member_f, axis=1, keepdims=True)
    inv_out[0] = jnp.broadcast_to(inv, inv_out.shape[1:])
    dst_pick = pick_rows(slots, dst_ref[row, :])
    links_out[0] = dot_nt(member, dst_pick).astype(BF16)
    gap_pick = pick_rows(table_ref.shape[0], gap_ref[row, :])
    gap_count = dot_nt(member, gap_pick).astype(BF16)
    code_mean = (dot(gap_count, table_ref[...]) * inv).astype(BF16)
    code_out[0] = dot(code_mean, w_code_ref[2 * DM :, :]).astype(BF16)


def ready_kernel(
    turn,
    at,
    me_ref,
    own_ref,
    memory_ref,
    touched_ref,
    touched_t_ref,
    w_msg_ref,
    w_hid_ref,
    links_ref,
    code_ref,
    inv_ref,
    *rest,
):
    outs = rest[turn > 1 : (turn > 1) + 7]
    total_out, inv_out, links_out, base_out, gh_out, held_out, kept_out = outs
    links_scr, code_scr, memory_scr, sems, snap_sem = rest[-5:]
    rows, touch, half = memory_ref.shape[0], touched_ref.shape[1], own_ref.shape[0]
    loads = copies(
        [
            (links_ref.at[at, :, :half], links_scr),
            (links_ref.at[at, :, half:], links_out),
            (code_ref.at[at], code_scr),
            (inv_ref.at[at], inv_out),
        ],
        sems,
    )
    for copy in loads:
        copy.start()
    memory = memory_ref[...]
    if turn > 0:
        snap_store = pltpu.make_async_copy(memory_scr, rest[-6], snap_sem)

        @pl.when(me_ref[0] == turn - 1)
        def _():
            memory_scr[...] = memory.astype(F32)
            snap_store.start()

    pick = same16(touched_t_ref[:, turn : turn + 1], iota((touch, rows), 1))
    held = dot(pick, memory).astype(BF16)
    held_out[...] = held
    gh_out[...] = dot(held, w_hid_ref[...])
    base = dot(held, w_msg_ref[:DM, :])
    now = touched_ref[turn : turn + 1, :]
    hit = dot(pick_rows(rows, now), jnp.ones((touch, 128), BF16))
    free = (1.0 - hit).astype(BF16)
    kept_out[...] = memory * jnp.concatenate([free, free], axis=1)
    loads[0].wait()
    total_out[...] = dot(links_scr[...], own_ref[...])
    loads[2].wait()
    base_out[...] = base + code_scr[...].astype(F32)
    loads[1].wait()
    loads[3].wait()
    if turn > 0:

        @pl.when(me_ref[0] == turn - 1)
        def _():
            snap_store.wait()


def updated(other, total, inv, links, base, gh, held, w_dst, w_in):
    raw = total + dot(links, other)
    raw = (raw * jnp.concatenate([inv, inv], axis=1)).astype(BF16)
    aggregate = (dot(raw, w_dst) + base).astype(BF16)
    gi = dot(aggregate, w_in)
    reset_gate = jax.nn.sigmoid(gi[:, :DM] + gh[:, :DM])
    update_gate = jax.nn.sigmoid(gi[:, DM : 2 * DM] + gh[:, DM : 2 * DM])
    candidate = jnp.tanh(gi[:, 2 * DM :] + reset_gate * gh[:, 2 * DM :])
    return (1.0 - update_gate) * candidate + update_gate * held.astype(F32)


def update_kernel(
    turn,
    me_ref,
    own_ref,
    other_ref,
    total_ref,
    inv_ref,
    links_ref,
    base_ref,
    gh_ref,
    held_ref,
    memory_ref,
    touched_ref,
    serve_t_ref,
    w_msg_ref,
    w_in_ref,
    *rest,
):
    memory_out, served_out, kept_out, fresh_kept_out, fresh_scr, kept_sems = rest[-6:]
    half, rows = own_ref.shape[0], memory_ref.shape[0]
    mine = me_ref[0] == turn
    keeps = copies(
        [
            (own_ref, kept_out.at[:half]),
            (other_ref, kept_out.at[half:]),
            (fresh_scr, fresh_kept_out),
        ],
        kept_sems,
    )

    @pl.when(mine)
    def _():
        for copy in keeps[:2]:
            copy.start()

    fresh = updated(
        other_ref[...],
        total_ref[...],
        inv_ref[...],
        links_ref[...],
        base_ref[...],
        gh_ref[...],
        held_ref[...],
        w_msg_ref[DM : 2 * DM, :],
        w_in_ref[...],
    ).astype(BF16)
    place = pick_rows(rows, touched_ref[turn : turn + 1, :])
    memory = memory_ref[...] + dot(place, fresh).astype(BF16)
    serve = same16(serve_t_ref[:, turn + 1 : turn + 2], iota((half, rows), 1))
    served_out[...] = dot(serve, memory).astype(BF16)
    memory_out[...] = memory

    @pl.when(mine)
    def _():
        fresh_scr[...] = fresh
        keeps[2].start()
        for copy in keeps:
            copy.wait()


def last_kernel(
    turn,
    me_ref,
    counts_ref,
    own_ref,
    other_ref,
    total_ref,
    inv_ref,
    links_ref,
    base_ref,
    gh_ref,
    held_ref,
    memory_ref,
    w_msg_ref,
    w_in_ref,
    touched_ref,
    nbr_ref,
    codes_ref,
    lists_ref,
    w_nbr_ref,
    w_out_ref,
    rows_ref,
    fresh_kept_ref,
    snap_in_ref,
    emb_out,
    snap_out,
    snap_scr,
    emb_scr,
    sems,
):
    mine = me_ref[0] == turn
    half = own_ref.shape[0]
    events = emb_scr.shape[0]
    rows, touch = memory_ref.shape[0], touched_ref.shape[1]
    snap_store = pltpu.make_async_copy(snap_scr, snap_out, sems.at[0])
    own = jnp.where(mine, own_ref[...], rows_ref[:half, :])
    other = jnp.where(mine, other_ref[...], rows_ref[half:, :])
    near = dot(nbr_ref[:, :half], own) + dot(nbr_ref[:, half:], other)
    hidden = dot(near.astype(BF16), w_nbr_ref[:DM, :]) + dot(codes_ref[...], w_nbr_ref[DM:, :])
    hidden = jnp.maximum(hidden, 0.0).astype(BF16)
    lower = dot(hidden, w_out_ref[DM:, :])
    fresh = updated(
        other_ref[...],
        total_ref[...],
        inv_ref[...],
        links_ref[...],
        base_ref[...],
        gh_ref[...],
        held_ref[...],
        w_msg_ref[DM : 2 * DM, :],
        w_in_ref[...],
    )
    place = pick_rows(rows, touched_ref[turn : turn + 1, :])
    high, low = split_two(fresh)
    snap_scr[...] = memory_ref[...].astype(F32) + (dot(place, high) + dot(place, low))

    @pl.when(mine)
    def _():
        snap_store.start()

    fresh = jnp.where(mine, high, fresh_kept_ref[...])
    block = events // 2
    stores = []
    for i in range(2):
        at = slice(i * block, (i + 1) * block)
        sources = lists_ref[at, 2 * NBRS : 2 * NBRS + 1]
        src_pick = same16(sources, iota((block, touch), 1))
        src_new = dot(src_pick, fresh).astype(BF16)
        out = dot(src_new, w_out_ref[:DM, :]) + lower[at, :]
        live = iota((block, 1), 0) + i * block < counts_ref[me_ref[0]]
        emb_scr[at, :] = jnp.where(live, out, 0.0).astype(BF16)
        store = pltpu.make_async_copy(emb_scr.at[at], emb_out.at[at], sems.at[1 + i])
        store.start()
        stores.append(store)

    @pl.when(mine)
    def _():
        snap_store.wait()

    for store in stores:
        store.wait()


def count_block(lists, number, begin, width):
    lanes = iota((lists.shape[0], width), 1)
    total = same16(lists[:, begin : begin + 1], lanes)
    for q in range(begin + 1, begin + number):
        total += same16(lists[:, q : q + 1], lanes)
    return total


def neighbours_kernel(after_ref, lists_ref, out_ref):
    block = 64

    def step(i, carry):
        at = pl.ds(pl.multiple_of(i * block, block), block)
        out_ref[at, :] = count_block(lists_ref[at, :], NBRS, 0, out_ref.shape[1])
        return carry

    lax.fori_loop(0, out_ref.shape[0] // block, step, 0)


def codes_kernel(after_ref, lists_ref, high_ref, low_ref, out_ref):
    block = 128

    def step(i, carry):
        at = pl.ds(pl.multiple_of(i * block, block), block)
        counts = count_block(lists_ref[at, :], NBRS, NBRS, high_ref.shape[0])
        out_ref[at, :] = (dot(counts, high_ref[...]) + dot(counts, low_ref[...])).astype(BF16)
        return carry

    lax.fori_loop(0, out_ref.shape[0] // block, step, 0)


def tie_kernel(*refs):
    pass


def in_hbm(dims, dtype):
    return pltpu.HBM(dims, dtype)


def stay(arrays):
    return [pltpu.with_memory_space_constraint(x, pltpu.HBM) for x in arrays]


def shape(dims, dtype):
    return jax.ShapeDtypeStruct(dims, dtype)


def params(mib=16):
    return pltpu.CompilerParams(vmem_limit_bytes=mib * 1024 * 1024)


def cost(flops, bytes_accessed):
    return pl.CostEstimate(flops=flops, bytes_accessed=bytes_accessed, transcendentals=0)


def body(
    memory,
    touched,
    src_slot,
    ev_count,
    serve_rows,
    dst_slot,
    nbr_slot,
    ev_gap,
    nbr_gap,
    time_freq,
    time_phase,
    w_msg,
    w_in,
    w_hid,
    w_nbr,
    w_out,
):
    me = lax.axis_index("tm")
    core = me % 2
    sections = lax.axis_size("tm")
    shards = lax.axis_size("node")
    rows = memory.shape[0]
    events = src_slot.shape[2]
    slots = serve_rows.shape[2]
    half = slots // 2
    capacity = slots // shards
    part = capacity // 2
    touched = touched[:, 0, :]
    touch = touched.shape[1]

    lists = [
        serve_rows.reshape(-1, 128),
        dst_slot.reshape(-1, 128),
        src_slot.reshape(-1, 128),
        ev_gap.reshape(-1, 128),
    ]
    lines = sum(x.shape[0] for x in lists) + 4
    packed = pl.pallas_call(
        pack_kernel,
        out_shape=shape((sections, lines, 128), jnp.int32),
        in_specs=[HBM] * 4 + [SMEM],
        out_specs=HBM,
        scratch_shapes=[
            pltpu.VMEM((lines, 128), jnp.int32),
            pltpu.SemaphoreType.DMA((4,)),
            pltpu.SemaphoreType.DMA((sections,)),
        ],
        compiler_params=params(),
        name="pack",
    )(*stay(lists), ev_count)
    everyone = lax.all_to_all(packed, "tm", split_axis=0, concat_axis=0, tiled=True).reshape(
        sections, -1
    )
    serve_all = everyone[:, :slots].reshape(sections, shards, 2, part)
    serve_own = jnp.where(core == 0, serve_all[:, :, 0], serve_all[:, :, 1])
    serve_t = serve_own.reshape(sections, half).T
    at = slots
    dst_all = everyone[:, at : at + events]
    at += events
    src_all = everyone[:, at : at + events]
    at += events
    gap_all = everyone[:, at : at + events]
    at += events
    count_all = everyone[:, at]

    def reordered(slot):
        place = slot % capacity
        mine = (place // part) == core
        return (slot // capacity) * part + place % part + jnp.where(mine, 0, half)

    dst_all = reordered(dst_all)
    touched_t = touched.T
    me_s = me.reshape(1).astype(jnp.int32)
    freq = jnp.pad(time_freq, (0, CODE - TD)).reshape(1, CODE)
    phase = jnp.pad(time_phase, (0, CODE - TD)).reshape(1, CODE)
    w_msg = jnp.pad(w_msg, ((0, CODE - TD), (0, 0)))
    w_nbr = jnp.pad(w_nbr, ((0, CODE - TD), (0, 0)))

    def call(kernel, name, outs, ins, operands, **more):
        return pl.pallas_call(
            kernel,
            out_shape=outs,
            in_specs=ins,
            compiler_params=params(),
            cost_estimate=cost(10**9, 2**22),
            name=name,
            **more,
        )(*operands)

    table, table_low = call(
        table_kernel,
        "table",
        (shape((GAPS, CODE), BF16),) * 2,
        [VMEM] * 2,
        (freq, phase),
        out_specs=(VMEM,) * 2,
    )
    served, memory_now = pl.pallas_call(
        first_serve_kernel,
        out_shape=(shape((half, DM), BF16), shape((rows, DM), BF16)),
        in_specs=[VMEM] * 2 + [ANY] * 2,
        out_specs=(VMEM,) * 2,
        compiler_params=params(),
        name="first_serve",
    )(serve_t, memory, touched, touched_t)

    def make_links(begin, number, after):
        return call(
            functools.partial(links_kernel, begin),
            "links",
            (
                in_hbm((number, touch, slots), BF16),
                in_hbm((number, touch, DM), BF16),
                in_hbm((number, touch, 128), F32),
            ),
            [HBM] + [VMEM] * 3 + [SMEM] + [VMEM] * 2,
            (*stay([after]), src_all, dst_all, gap_all, count_all, table, w_msg),
            out_specs=(
                pl.BlockSpec((1, touch, slots), lambda t: (t, 0, 0)),
                pl.BlockSpec((1, touch, DM), lambda t: (t, 0, 0)),
                pl.BlockSpec((1, touch, 128), lambda t: (t, 0, 0)),
            ),
            grid=(number,),
        )

    split = min(FIRST, sections)
    parts = [make_links(0, split, memory)]
    lists_t = jnp.concatenate(
        [reordered(nbr_slot[0, 0]), nbr_gap[0, 0], src_slot.reshape(1, events)], axis=0
    ).T
    snap, keeps = (), ()
    swap = [(i, i ^ 1) for i in range(sections)]
    for turn in range(sections):
        own = lax.all_to_all(
            served.reshape(shards, part, DM), "node", split_axis=0, concat_axis=0, tiled=True
        ).reshape(half, DM)
        if turn == 1:
            nbr_counts = call(
                neighbours_kernel,
                "neighbour_counts",
                in_hbm((events, slots), BF16),
                [HBM, VMEM],
                (*stay([memory_now]), lists_t),
                out_specs=VMEM,
            )
            nbr_codes = call(
                codes_kernel,
                "codes",
                in_hbm((events, CODE), BF16),
                [HBM] + [VMEM] * 3,
                (*stay([memory_now]), lists_t, table, table_low),
                out_specs=VMEM,
            )
            parts.append(make_links(split, sections - split, memory_now))
        if turn < 2:
            beside = stay([parts[0][0]] if turn == 0 else [nbr_counts, nbr_codes, parts[1][0]])
            own = pl.pallas_call(
                tie_kernel,
                out_shape=shape(own.shape, own.dtype),
                in_specs=[ANY] + [HBM] * len(beside),
                out_specs=ANY,
                input_output_aliases={0: 0},
                compiler_params=params(1),
                name="tie",
            )(own, *beside)
        other = lax.ppermute(own, "tm", swap)
        late_links = turn >= split
        outs = call(
            functools.partial(ready_kernel, turn, turn - split * late_links),
            "ready",
            (
                shape((touch, DM), F32),
                shape((touch, 128), F32),
                shape((touch, half), BF16),
                shape((touch, DM), F32),
                shape((touch, 3 * DM), F32),
                shape((touch, DM), BF16),
                shape((rows, DM), BF16),
            )
            + (in_hbm((rows, DM), F32),) * (turn > 0),
            [SMEM] + [VMEM] * 6 + [HBM] * (3 + len(snap)),
            (
                me_s,
                own,
                memory_now,
                touched,
                touched_t,
                w_msg,
                w_hid,
                *stay((*parts[late_links], *snap)),
            ),
            out_specs=(VMEM,) * 7 + (HBM,) * (turn > 0),
            scratch_shapes=[
                pltpu.VMEM((touch, half), BF16),
                pltpu.VMEM((touch, DM), BF16),
                pltpu.VMEM((rows, DM), F32),
                pltpu.SemaphoreType.DMA((4,)),
                pltpu.SemaphoreType.DMA,
            ],
            input_output_aliases={10: 7} if snap else {},
        )
        ready, snap = outs[:7], outs[7:]
        if turn + 1 == sections:
            break
        memory_now, served, *keeps = call(
            functools.partial(update_kernel, turn),
            "update",
            (
                (in_hbm if turn == 0 else shape)((rows, DM), BF16),
                shape((half, DM), BF16),
                in_hbm((slots, DM), BF16),
                in_hbm((touch, DM), BF16),
            ),
            [SMEM] + [VMEM] * 13 + [HBM] * len(keeps),
            (me_s, own, other, *ready, touched, serve_t, w_msg, w_in, *stay(keeps)),
            out_specs=(VMEM,) * 2 + (HBM,) * 2,
            scratch_shapes=[pltpu.VMEM((touch, DM), BF16), pltpu.SemaphoreType.DMA((3,))],
            input_output_aliases={14: 2, 15: 3} if keeps else {},
        )
    late = (nbr_counts, nbr_codes, lists_t, w_nbr, w_out)
    emb, snap = call(
        functools.partial(last_kernel, turn),
        "last",
        (in_hbm((events, DM), BF16), in_hbm((rows, DM), F32)),
        [SMEM] * 2 + [VMEM] * 19 + [HBM],
        (
            me_s,
            count_all,
            own,
            other,
            *ready,
            w_msg,
            w_in,
            touched,
            *late,
            *keeps,
            *stay(snap),
        ),
        out_specs=(HBM,) * 2,
        scratch_shapes=[
            pltpu.VMEM((rows, DM), F32),
            pltpu.VMEM((events, DM), BF16),
            pltpu.SemaphoreType.DMA((3,)),
        ],
        input_output_aliases={21: 1},
    )
    return (emb[None, None], snap[None])


def solution(mesh):
    return jax.shard_map(
        body,
        mesh=mesh,
        in_specs=(
            P("node", None),
            P(None, "node", None),
            P("tm", "node", None),
            P("tm", "node"),
            P("tm", "node", None),
            P("tm", "node", None),
            P("tm", "node", None, None),
            P("tm", "node", None),
            P("tm", "node", None, None),
            P(),
            P(),
            P(),
            P(),
            P(),
            P(),
            P(),
        ),
        out_specs=(P("tm", "node", None, None), P("tm", "node", None)),
        check_vma=False,
    )
```

```python
import functools

import jax
import jax.numpy as jnp
from jax import lax
from jax.experimental import pallas as pl
from jax.experimental.pallas import tpu as pltpu
from jax.sharding import PartitionSpec as P

DM = 256
TD = 100
CODE = 128
GAPS = 1024
NBRS = 10
FIRST = 6
F32 = jnp.float32
BF16 = jnp.bfloat16
VMEM = pl.BlockSpec(memory_space=pltpu.VMEM)
SMEM = pl.BlockSpec(memory_space=pltpu.SMEM)
ANY = pl.BlockSpec(memory_space=pl.ANY)
HBM = pl.BlockSpec(memory_space=pltpu.HBM)


def dot(a, b):
    return jnp.dot(a, b, preferred_element_type=F32)


def dot_nt(a, b):
    return lax.dot_general(a, b, (((1,), (1,)), ((), ())), preferred_element_type=F32)


def iota(shape, axis):
    return lax.broadcasted_iota(jnp.int32, shape, axis)


def same16(a, b):
    mask = a.astype(jnp.int16) == b.astype(jnp.int16)
    return jnp.where(mask, jnp.ones((), BF16), jnp.zeros((), BF16))


def pick_rows(height, row):
    row = row.astype(jnp.int16)
    base = iota((16, row.shape[1]), 0).astype(jnp.int16)
    one, zero = jnp.ones((), BF16), jnp.zeros((), BF16)
    return jnp.concatenate(
        [jnp.where(base + jnp.int16(i) == row, one, zero) for i in range(0, height, 16)], axis=0
    )


def split_two(x):
    high = x.astype(BF16)
    return high, (x - high.astype(F32)).astype(BF16)


def copies(pairs, sems):
    return [pltpu.make_async_copy(src, dst, sems.at[i]) for i, (src, dst) in enumerate(pairs)]


def pack_kernel(serve_ref, dst_ref, src_ref, gap_ref, count_ref, out_ref, scr, in_sems, out_sems):
    at, pairs = 0, []
    for ref in (serve_ref, dst_ref, src_ref, gap_ref):
        pairs.append((ref, scr.at[at : at + ref.shape[0]]))
        at += ref.shape[0]
    loads = copies(pairs, in_sems)
    for copy in loads:
        copy.start()
    scr[at:, :] = jnp.full((scr.shape[0] - at, 128), count_ref[0, 0], jnp.int32)
    for copy in loads:
        copy.wait()
    sends = copies([(scr, out_ref.at[i]) for i in range(out_ref.shape[0])], out_sems)
    for copy in sends:
        copy.start()
    for copy in sends:
        copy.wait()


def first_serve_kernel(serve_ref, memory_ref, *rest):
    served_out, memory_out = rest[-2:]
    memory = memory_ref[...].astype(BF16)
    memory_out[...] = memory
    pick = same16(serve_ref[:, 0:1], iota((serve_ref.shape[0], memory.shape[0]), 1))
    served_out[...] = dot(pick, memory).astype(BF16)


def table_kernel(freq_ref, phase_ref, high_out, low_out):
    gap = iota(high_out.shape, 0).astype(F32)
    high, low = split_two(jnp.cos(gap * freq_ref[...] + phase_ref[...]))
    high_out[...] = high
    low_out[...] = low


def links_kernel(begin, after_ref, src_ref, dst_ref, gap_ref, count_ref, table_ref, w_code_ref, links_out, code_out, inv_out):
    turn = begin + pl.program_id(0)
    touch, slots = links_out.shape[1:]
    events = src_ref.shape[1]
    row = pl.ds(turn, 1)
    live = iota((touch, events), 1) < count_ref[turn]
    member_mask = jnp.logical_and(iota((touch, events), 0) == src_ref[row, :], live)
    member_f = jnp.where(member_mask, 1.0, 0.0)
    member = member_f.astype(BF16)
    inv = 1.0 / jnp.sum(member_f, axis=1, keepdims=True)
    inv_out[0] = jnp.broadcast_to(inv, inv_out.shape[1:])
    dst_pick = pick_rows(slots, dst_ref[row, :])
    links_out[0] = dot_nt(member, dst_pick).astype(BF16)
    gap_pick = pick_rows(table_ref.shape[0], gap_ref[row, :])
    gap_count = dot_nt(member, gap_pick).astype(BF16)
    code_mean = (dot(gap_count, table_ref[...]) * inv).astype(BF16)
    code_out[0] = dot(code_mean, w_code_ref[2 * DM :, :]).astype(BF16)


def ready_kernel(
    turn,
    at,
    me_ref,
    own_ref,
    memory_ref,
    touched_ref,
    touched_t_ref,
    w_msg_ref,
    w_hid_ref,
    links_ref,
    code_ref,
    inv_ref,
    *rest,
):
    outs = rest[turn > 1 : (turn > 1) + 7]
    total_out, inv_out, links_out, base_out, gh_out, held_out, kept_out = outs
    links_scr, code_scr, memory_scr, sems, snap_sem = rest[-5:]
    rows, touch, half = memory_ref.shape[0], touched_ref.shape[1], own_ref.shape[0]
    loads = copies(
        [
            (links_ref.at[at, :, :half], links_scr),
            (links_ref.at[at, :, half:], links_out),
            (code_ref.at[at], code_scr),
            (inv_ref.at[at], inv_out),
        ],
        sems,
    )
    for copy in loads:
        copy.start()
    memory = memory_ref[...]
    if turn > 0:
        snap_store = pltpu.make_async_copy(memory_scr, rest[-6], snap_sem)

        @pl.when(me_ref[0] == turn - 1)
        def _():
            memory_scr[...] = memory.astype(F32)
            snap_store.start()

    pick = same16(touched_t_ref[:, turn : turn + 1], iota((touch, rows), 1))
    held = dot(pick, memory).astype(BF16)
    held_out[...] = held
    gh_out[...] = dot(held, w_hid_ref[...])
    base = dot(held, w_msg_ref[:DM, :])
    now = touched_ref[turn : turn + 1, :]
    hit = dot(pick_rows(rows, now), jnp.ones((touch, 128), BF16))
    free = (1.0 - hit).astype(BF16)
    kept_out[...] = memory * jnp.concatenate([free, free], axis=1)
    loads[0].wait()
    total_out[...] = dot(links_scr[...], own_ref[...])
    loads[2].wait()
    base_out[...] = base + code_scr[...].astype(F32)
    loads[1].wait()
    loads[3].wait()
    if turn > 0:

        @pl.when(me_ref[0] == turn - 1)
        def _():
            snap_store.wait()


def updated(other, total, inv, links, base, gh, held, w_dst, w_in):
    raw = total + dot(links, other)
    raw = (raw * jnp.concatenate([inv, inv], axis=1)).astype(BF16)
    aggregate = (dot(raw, w_dst) + base).astype(BF16)
    gi = dot(aggregate, w_in)
    reset_gate = jax.nn.sigmoid(gi[:, :DM] + gh[:, :DM])
    update_gate = jax.nn.sigmoid(gi[:, DM : 2 * DM] + gh[:, DM : 2 * DM])
    candidate = jnp.tanh(gi[:, 2 * DM :] + reset_gate * gh[:, 2 * DM :])
    return (1.0 - update_gate) * candidate + update_gate * held.astype(F32)


def update_kernel(
    turn,
    me_ref,
    own_ref,
    other_ref,
    total_ref,
    inv_ref,
    links_ref,
    base_ref,
    gh_ref,
    held_ref,
    memory_ref,
    touched_ref,
    serve_t_ref,
    w_msg_ref,
    w_in_ref,
    *rest,
):
    memory_out, served_out, kept_out, fresh_kept_out, fresh_scr, kept_sems = rest[-6:]
    half, rows = own_ref.shape[0], memory_ref.shape[0]
    mine = me_ref[0] == turn
    keeps = copies(
        [
            (own_ref, kept_out.at[:half]),
            (other_ref, kept_out.at[half:]),
            (fresh_scr, fresh_kept_out),
        ],
        kept_sems,
    )

    @pl.when(mine)
    def _():
        for copy in keeps[:2]:
            copy.start()

    fresh = updated(
        other_ref[...],
        total_ref[...],
        inv_ref[...],
        links_ref[...],
        base_ref[...],
        gh_ref[...],
        held_ref[...],
        w_msg_ref[DM : 2 * DM, :],
        w_in_ref[...],
    ).astype(BF16)
    place = pick_rows(rows, touched_ref[turn : turn + 1, :])
    memory = memory_ref[...] + dot(place, fresh).astype(BF16)
    serve = same16(serve_t_ref[:, turn + 1 : turn + 2], iota((half, rows), 1))
    served_out[...] = dot(serve, memory).astype(BF16)
    memory_out[...] = memory

    @pl.when(mine)
    def _():
        fresh_scr[...] = fresh
        keeps[2].start()
        for copy in keeps:
            copy.wait()


def last_kernel(
    turn,
    me_ref,
    counts_ref,
    own_ref,
    other_ref,
    total_ref,
    inv_ref,
    links_ref,
    base_ref,
    gh_ref,
    held_ref,
    memory_ref,
    w_msg_ref,
    w_in_ref,
    touched_ref,
    nbr_ref,
    codes_ref,
    lists_ref,
    w_nbr_ref,
    w_out_ref,
    rows_ref,
    fresh_kept_ref,
    snap_in_ref,
    emb_out,
    snap_out,
    snap_scr,
    emb_scr,
    sems,
):
    mine = me_ref[0] == turn
    half = own_ref.shape[0]
    events = emb_scr.shape[0]
    rows, touch = memory_ref.shape[0], touched_ref.shape[1]
    snap_store = pltpu.make_async_copy(snap_scr, snap_out, sems.at[0])
    own = jnp.where(mine, own_ref[...], rows_ref[:half, :])
    other = jnp.where(mine, other_ref[...], rows_ref[half:, :])
    near = dot(nbr_ref[:, :half], own) + dot(nbr_ref[:, half:], other)
    hidden = dot(near.astype(BF16), w_nbr_ref[:DM, :]) + dot(codes_ref[...], w_nbr_ref[DM:, :])
    hidden = jnp.maximum(hidden, 0.0).astype(BF16)
    lower = dot(hidden, w_out_ref[DM:, :])
    fresh = updated(
        other_ref[...],
        total_ref[...],
        inv_ref[...],
        links_ref[...],
        base_ref[...],
        gh_ref[...],
        held_ref[...],
        w_msg_ref[DM : 2 * DM, :],
        w_in_ref[...],
    )
    place = pick_rows(rows, touched_ref[turn : turn + 1, :])
    high, low = split_two(fresh)
    snap_scr[...] = memory_ref[...].astype(F32) + (dot(place, high) + dot(place, low))

    @pl.when(mine)
    def _():
        snap_store.start()

    fresh = jnp.where(mine, high, fresh_kept_ref[...])
    block = events // 2
    stores = []
    for i in range(2):
        at = slice(i * block, (i + 1) * block)
        sources = lists_ref[at, 2 * NBRS : 2 * NBRS + 1]
        src_pick = same16(sources, iota((block, touch), 1))
        src_new = dot(src_pick, fresh).astype(BF16)
        out = dot(src_new, w_out_ref[:DM, :]) + lower[at, :]
        live = iota((block, 1), 0) + i * block < counts_ref[me_ref[0]]
        emb_scr[at, :] = jnp.where(live, out, 0.0).astype(BF16)
        store = pltpu.make_async_copy(emb_scr.at[at], emb_out.at[at], sems.at[1 + i])
        store.start()
        stores.append(store)

    @pl.when(mine)
    def _():
        snap_store.wait()

    for store in stores:
        store.wait()


def count_block(lists, number, begin, width):
    lanes = iota((lists.shape[0], width), 1)
    total = same16(lists[:, begin : begin + 1], lanes)
    for q in range(begin + 1, begin + number):
        total += same16(lists[:, q : q + 1], lanes)
    return total


def neighbours_kernel(after_ref, lists_ref, out_ref):
    block = 64

    def step(i, carry):
        at = pl.ds(pl.multiple_of(i * block, block), block)
        out_ref[at, :] = count_block(lists_ref[at, :], NBRS, 0, out_ref.shape[1])
        return carry

    lax.fori_loop(0, out_ref.shape[0] // block, step, 0)


def codes_kernel(after_ref, lists_ref, high_ref, low_ref, out_ref):
    block = 128

    def step(i, carry):
        at = pl.ds(pl.multiple_of(i * block, block), block)
        counts = count_block(lists_ref[at, :], NBRS, NBRS, high_ref.shape[0])
        out_ref[at, :] = (dot(counts, high_ref[...]) + dot(counts, low_ref[...])).astype(BF16)
        return carry

    lax.fori_loop(0, out_ref.shape[0] // block, step, 0)


def tie_kernel(*refs):
    pass


def in_hbm(dims, dtype):
    return pltpu.HBM(dims, dtype)


def stay(arrays):
    return [pltpu.with_memory_space_constraint(x, pltpu.HBM) for x in arrays]


def shape(dims, dtype):
    return jax.ShapeDtypeStruct(dims, dtype)


def params(mib=16):
    return pltpu.CompilerParams(vmem_limit_bytes=mib * 1024 * 1024)


def cost(flops, bytes_accessed):
    return pl.CostEstimate(flops=flops, bytes_accessed=bytes_accessed, transcendentals=0)


def body(
    memory,
    touched,
    src_slot,
    ev_count,
    serve_rows,
    dst_slot,
    nbr_slot,
    ev_gap,
    nbr_gap,
    time_freq,
    time_phase,
    w_msg,
    w_in,
    w_hid,
    w_nbr,
    w_out,
):
    me = lax.axis_index("tm")
    core = me % 2
    sections = lax.axis_size("tm")
    shards = lax.axis_size("node")
    rows = memory.shape[0]
    events = src_slot.shape[2]
    slots = serve_rows.shape[2]
    half = slots // 2
    capacity = slots // shards
    part = capacity // 2
    touched = touched[:, 0, :]
    touch = touched.shape[1]

    lists = [
        serve_rows.reshape(-1, 128),
        dst_slot.reshape(-1, 128),
        src_slot.reshape(-1, 128),
        ev_gap.reshape(-1, 128),
    ]
    lines = sum(x.shape[0] for x in lists) + 4
    packed = pl.pallas_call(
        pack_kernel,
        out_shape=shape((sections, lines, 128), jnp.int32),
        in_specs=[HBM] * 4 + [SMEM],
        out_specs=HBM,
        scratch_shapes=[
            pltpu.VMEM((lines, 128), jnp.int32),
            pltpu.SemaphoreType.DMA((4,)),
            pltpu.SemaphoreType.DMA((sections,)),
        ],
        compiler_params=params(),
        name="pack",
    )(*stay(lists), ev_count)
    everyone = lax.all_to_all(packed, "tm", split_axis=0, concat_axis=0, tiled=True).reshape(
        sections, -1
    )
    serve_all = everyone[:, :slots].reshape(sections, shards, 2, part)
    serve_own = jnp.where(core == 0, serve_all[:, :, 0], serve_all[:, :, 1])
    serve_t = serve_own.reshape(sections, half).T
    at = slots
    dst_all = everyone[:, at : at + events]
    at += events
    src_all = everyone[:, at : at + events]
    at += events
    gap_all = everyone[:, at : at + events]
    at += events
    count_all = everyone[:, at]

    def reordered(slot):
        place = slot % capacity
        mine = (place // part) == core
        return (slot // capacity) * part + place % part + jnp.where(mine, 0, half)

    dst_all = reordered(dst_all)
    touched_t = touched.T
    me_s = me.reshape(1).astype(jnp.int32)
    freq = jnp.pad(time_freq, (0, CODE - TD)).reshape(1, CODE)
    phase = jnp.pad(time_phase, (0, CODE - TD)).reshape(1, CODE)
    w_msg = jnp.pad(w_msg, ((0, CODE - TD), (0, 0)))
    w_nbr = jnp.pad(w_nbr, ((0, CODE - TD), (0, 0)))

    def call(kernel, name, outs, ins, operands, **more):
        return pl.pallas_call(
            kernel,
            out_shape=outs,
            in_specs=ins,
            compiler_params=params(),
            cost_estimate=cost(10**9, 2**22),
            name=name,
            **more,
        )(*operands)

    table, table_low = call(
        table_kernel,
        "table",
        (shape((GAPS, CODE), BF16),) * 2,
        [VMEM] * 2,
        (freq, phase),
        out_specs=(VMEM,) * 2,
    )
    served, memory_now = pl.pallas_call(
        first_serve_kernel,
        out_shape=(shape((half, DM), BF16), shape((rows, DM), BF16)),
        in_specs=[VMEM] * 2 + [ANY] * 4,
        out_specs=(VMEM,) * 2,
        compiler_params=params(),
        name="first_serve",
    )(serve_t, memory, touched, touched_t, table, w_msg)

    def make_links(begin, number, after):
        return call(
            functools.partial(links_kernel, begin),
            "links",
            (
                in_hbm((number, touch, slots), BF16),
                in_hbm((number, touch, DM), BF16),
                in_hbm((number, touch, 128), F32),
            ),
            [HBM] + [VMEM] * 3 + [SMEM] + [VMEM] * 2,
            (*stay([after]), src_all, dst_all, gap_all, count_all, table, w_msg),
            out_specs=(
                pl.BlockSpec((1, touch, slots), lambda t: (t, 0, 0)),
                pl.BlockSpec((1, touch, DM), lambda t: (t, 0, 0)),
                pl.BlockSpec((1, touch, 128), lambda t: (t, 0, 0)),
            ),
            grid=(number,),
        )

    split = min(FIRST, sections)
    parts = [make_links(0, split, memory)]
    lists_t = jnp.concatenate(
        [reordered(nbr_slot[0, 0]), nbr_gap[0, 0], src_slot.reshape(1, events)], axis=0
    ).T
    snap, keeps = (), ()
    swap = [(i, i ^ 1) for i in range(sections)]
    for turn in range(sections):
        own = lax.all_to_all(
            served.reshape(shards, part, DM), "node", split_axis=0, concat_axis=0, tiled=True
        ).reshape(half, DM)
        if turn == 1:
            nbr_counts = call(
                neighbours_kernel,
                "neighbour_counts",
                in_hbm((events, slots), BF16),
                [HBM, VMEM],
                (*stay([memory_now]), lists_t),
                out_specs=VMEM,
            )
            nbr_codes = call(
                codes_kernel,
                "codes",
                in_hbm((events, CODE), BF16),
                [HBM] + [VMEM] * 3,
                (*stay([memory_now]), lists_t, table, table_low),
                out_specs=VMEM,
            )
            parts.append(make_links(split, sections - split, memory_now))
        if turn < 2:
            beside = stay([parts[0][0]] if turn == 0 else [nbr_counts, nbr_codes, parts[1][0]])
            own = pl.pallas_call(
                tie_kernel,
                out_shape=shape(own.shape, own.dtype),
                in_specs=[ANY] + [HBM] * len(beside),
                out_specs=ANY,
                input_output_aliases={0: 0},
                compiler_params=params(1),
                name="tie",
            )(own, *beside)
        other = lax.ppermute(own, "tm", swap)
        late_links = turn >= split
        outs = call(
            functools.partial(ready_kernel, turn, turn - split * late_links),
            "ready",
            (
                shape((touch, DM), F32),
                shape((touch, 128), F32),
                shape((touch, half), BF16),
                shape((touch, DM), F32),
                shape((touch, 3 * DM), F32),
                shape((touch, DM), BF16),
                shape((rows, DM), BF16),
            )
            + (in_hbm((rows, DM), F32),) * (turn > 0),
            [SMEM] + [VMEM] * 6 + [HBM] * (3 + len(snap)),
            (
                me_s,
                own,
                memory_now,
                touched,
                touched_t,
                w_msg,
                w_hid,
                *stay((*parts[late_links], *snap)),
            ),
            out_specs=(VMEM,) * 7 + (HBM,) * (turn > 0),
            scratch_shapes=[
                pltpu.VMEM((touch, half), BF16),
                pltpu.VMEM((touch, DM), BF16),
                pltpu.VMEM((rows, DM), F32),
                pltpu.SemaphoreType.DMA((4,)),
                pltpu.SemaphoreType.DMA,
            ],
            input_output_aliases={10: 7} if snap else {},
        )
        ready, snap = outs[:7], outs[7:]
        if turn + 1 == sections:
            break
        memory_now, served, *keeps = call(
            functools.partial(update_kernel, turn),
            "update",
            (
                (in_hbm if turn == 0 else shape)((rows, DM), BF16),
                shape((half, DM), BF16),
                in_hbm((slots, DM), BF16),
                in_hbm((touch, DM), BF16),
            ),
            [SMEM] + [VMEM] * 13 + [HBM] * len(keeps),
            (me_s, own, other, *ready, touched, serve_t, w_msg, w_in, *stay(keeps)),
            out_specs=(VMEM,) * 2 + (HBM,) * 2,
            scratch_shapes=[pltpu.VMEM((touch, DM), BF16), pltpu.SemaphoreType.DMA((3,))],
            input_output_aliases={14: 2, 15: 3} if keeps else {},
        )
    late = (nbr_counts, nbr_codes, lists_t, w_nbr, w_out)
    emb, snap = call(
        functools.partial(last_kernel, turn),
        "last",
        (in_hbm((events, DM), BF16), in_hbm((rows, DM), F32)),
        [SMEM] * 2 + [VMEM] * 19 + [HBM],
        (
            me_s,
            count_all,
            own,
            other,
            *ready,
            w_msg,
            w_in,
            touched,
            *late,
            *keeps,
            *stay(snap),
        ),
        out_specs=(HBM,) * 2,
        scratch_shapes=[
            pltpu.VMEM((rows, DM), F32),
            pltpu.VMEM((events, DM), BF16),
            pltpu.SemaphoreType.DMA((3,)),
        ],
        input_output_aliases={21: 1},
    )
    return (emb[None, None], snap[None])


def solution(mesh):
    return jax.shard_map(
        body,
        mesh=mesh,
        in_specs=(
            P("node", None),
            P(None, "node", None),
            P("tm", "node", None),
            P("tm", "node"),
            P("tm", "node", None),
            P("tm", "node", None),
            P("tm", "node", None, None),
            P("tm", "node", None),
            P("tm", "node", None, None),
            P(),
            P(),
            P(),
            P(),
            P(),
            P(),
            P(),
        ),
        out_specs=(P("tm", "node", None, None), P("tm", "node", None)),
        check_vma=False,
    )
```

```python
import functools

import jax
import jax.numpy as jnp
from jax import lax
from jax.experimental import pallas as pl
from jax.experimental.pallas import tpu as pltpu
from jax.sharding import PartitionSpec as P

DM = 256
TD = 100
CODE = 128
GAPS = 1024
NBRS = 10
FIRST = 6
F32 = jnp.float32
BF16 = jnp.bfloat16
VMEM = pl.BlockSpec(memory_space=pltpu.VMEM)
SMEM = pl.BlockSpec(memory_space=pltpu.SMEM)
ANY = pl.BlockSpec(memory_space=pl.ANY)
HBM = pl.BlockSpec(memory_space=pltpu.HBM)


def dot(a, b):
    return jnp.dot(a, b, preferred_element_type=F32)


def dot_nt(a, b):
    return lax.dot_general(a, b, (((1,), (1,)), ((), ())), preferred_element_type=F32)


def iota(shape, axis):
    return lax.broadcasted_iota(jnp.int32, shape, axis)


def same16(a, b):
    mask = a.astype(jnp.int16) == b.astype(jnp.int16)
    return jnp.where(mask, jnp.ones((), BF16), jnp.zeros((), BF16))


def pick_rows(height, row):
    row = row.astype(jnp.int16)
    base = iota((16, row.shape[1]), 0).astype(jnp.int16)
    one, zero = jnp.ones((), BF16), jnp.zeros((), BF16)
    return jnp.concatenate(
        [jnp.where(base + jnp.int16(i) == row, one, zero) for i in range(0, height, 16)], axis=0
    )


def split_two(x):
    high = x.astype(BF16)
    return high, (x - high.astype(F32)).astype(BF16)


def copies(pairs, sems):
    return [pltpu.make_async_copy(src, dst, sems.at[i]) for i, (src, dst) in enumerate(pairs)]


def pack_kernel(serve_ref, dst_ref, src_ref, gap_ref, count_ref, out_ref, scr, in_sems, out_sems):
    at, pairs = 0, []
    for ref in (serve_ref, dst_ref, src_ref, gap_ref):
        pairs.append((ref, scr.at[at : at + ref.shape[0]]))
        at += ref.shape[0]
    loads = copies(pairs, in_sems)
    for copy in loads:
        copy.start()
    scr[at:, :] = jnp.full((scr.shape[0] - at, 128), count_ref[0, 0], jnp.int32)
    for copy in loads:
        copy.wait()
    sends = copies([(scr, out_ref.at[i]) for i in range(out_ref.shape[0])], out_sems)
    for copy in sends:
        copy.start()
    for copy in sends:
        copy.wait()


def first_serve_kernel(serve_ref, memory_ref, *rest):
    served_out, memory_out = rest[-2:]
    memory = memory_ref[...].astype(BF16)
    memory_out[...] = memory
    pick = same16(serve_ref[:, 0:1], iota((serve_ref.shape[0], memory.shape[0]), 1))
    served_out[...] = dot(pick, memory).astype(BF16)


def table_kernel(freq_ref, phase_ref, high_out, low_out):
    gap = iota(high_out.shape, 0).astype(F32)
    high, low = split_two(jnp.cos(gap * freq_ref[...] + phase_ref[...]))
    high_out[...] = high
    low_out[...] = low


def links_kernel(begin, after_ref, src_ref, dst_ref, gap_ref, count_ref, table_ref, w_code_ref, touched_ref, links_out, code_out, inv_out, free_out):
    turn = begin + pl.program_id(0)
    touch, slots = links_out.shape[1:]
    events = src_ref.shape[1]
    row = pl.ds(turn, 1)
    live = iota((touch, events), 1) < count_ref[turn]
    member_mask = jnp.logical_and(iota((touch, events), 0) == src_ref[row, :], live)
    member_f = jnp.where(member_mask, 1.0, 0.0)
    member = member_f.astype(BF16)
    inv = 1.0 / jnp.sum(member_f, axis=1, keepdims=True)
    hit = dot(pick_rows(free_out.shape[1], touched_ref[row, :]), jnp.ones((touch, 128), BF16))
    free_out[0] = (1.0 - hit).astype(BF16)
    inv_out[0] = jnp.broadcast_to(inv, inv_out.shape[1:])
    dst_pick = pick_rows(slots, dst_ref[row, :])
    links_out[0] = dot_nt(member, dst_pick).astype(BF16)
    gap_pick = pick_rows(table_ref.shape[0], gap_ref[row, :])
    gap_count = dot_nt(member, gap_pick).astype(BF16)
    code_mean = (dot(gap_count, table_ref[...]) * inv).astype(BF16)
    code_out[0] = dot(code_mean, w_code_ref[2 * DM :, :]).astype(BF16)


def ready_kernel(
    turn,
    at,
    me_ref,
    own_ref,
    memory_ref,
    touched_ref,
    touched_t_ref,
    w_msg_ref,
    w_hid_ref,
    links_ref,
    code_ref,
    inv_ref,
    free_ref,
    *rest,
):
    outs = rest[turn > 1 : (turn > 1) + 7]
    total_out, inv_out, links_out, base_out, gh_out, held_out, kept_out = outs
    links_scr, code_scr, free_scr, memory_scr, sems, snap_sem = rest[-6:]
    rows, touch, half = memory_ref.shape[0], touched_ref.shape[1], own_ref.shape[0]
    loads = copies(
        [
            (links_ref.at[at, :, :half], links_scr),
            (links_ref.at[at, :, half:], links_out),
            (code_ref.at[at], code_scr),
            (inv_ref.at[at], inv_out),
            (free_ref.at[at], free_scr),
        ],
        sems,
    )
    for copy in loads:
        copy.start()
    memory = memory_ref[...]
    if turn > 0:
        snap_store = pltpu.make_async_copy(memory_scr, rest[-7], snap_sem)

        @pl.when(me_ref[0] == turn - 1)
        def _():
            memory_scr[...] = memory.astype(F32)
            snap_store.start()

    pick = same16(touched_t_ref[:, turn : turn + 1], iota((touch, rows), 1))
    held = dot(pick, memory).astype(BF16)
    held_out[...] = held
    gh_out[...] = dot(held, w_hid_ref[...])
    base = dot(held, w_msg_ref[:DM, :])
    loads[4].wait()
    free = free_scr[...]
    kept_out[...] = memory * jnp.concatenate([free, free], axis=1)
    loads[0].wait()
    total_out[...] = dot(links_scr[...], own_ref[...])
    loads[2].wait()
    base_out[...] = base + code_scr[...].astype(F32)
    loads[1].wait()
    loads[3].wait()
    if turn > 0:

        @pl.when(me_ref[0] == turn - 1)
        def _():
            snap_store.wait()


def updated(other, total, inv, links, base, gh, held, w_dst, w_in):
    raw = total + dot(links, other)
    raw = (raw * jnp.concatenate([inv, inv], axis=1)).astype(BF16)
    aggregate = (dot(raw, w_dst) + base).astype(BF16)
    gi = dot(aggregate, w_in)
    reset_gate = jax.nn.sigmoid(gi[:, :DM] + gh[:, :DM])
    update_gate = jax.nn.sigmoid(gi[:, DM : 2 * DM] + gh[:, DM : 2 * DM])
    candidate = jnp.tanh(gi[:, 2 * DM :] + reset_gate * gh[:, 2 * DM :])
    return (1.0 - update_gate) * candidate + update_gate * held.astype(F32)


def update_kernel(
    turn,
    me_ref,
    own_ref,
    other_ref,
    total_ref,
    inv_ref,
    links_ref,
    base_ref,
    gh_ref,
    held_ref,
    memory_ref,
    touched_ref,
    serve_t_ref,
    w_msg_ref,
    w_in_ref,
    *rest,
):
    memory_out, served_out, kept_out, fresh_kept_out, fresh_scr, kept_sems = rest[-6:]
    half, rows = own_ref.shape[0], memory_ref.shape[0]
    mine = me_ref[0] == turn
    keeps = copies(
        [
            (own_ref, kept_out.at[:half]),
            (other_ref, kept_out.at[half:]),
            (fresh_scr, fresh_kept_out),
        ],
        kept_sems,
    )

    @pl.when(mine)
    def _():
        for copy in keeps[:2]:
            copy.start()

    fresh = updated(
        other_ref[...],
        total_ref[...],
        inv_ref[...],
        links_ref[...],
        base_ref[...],
        gh_ref[...],
        held_ref[...],
        w_msg_ref[DM : 2 * DM, :],
        w_in_ref[...],
    ).astype(BF16)
    place = pick_rows(rows, touched_ref[turn : turn + 1, :])
    memory = memory_ref[...] + dot(place, fresh).astype(BF16)
    serve = same16(serve_t_ref[:, turn + 1 : turn + 2], iota((half, rows), 1))
    served_out[...] = dot(serve, memory).astype(BF16)
    memory_out[...] = memory

    @pl.when(mine)
    def _():
        fresh_scr[...] = fresh
        keeps[2].start()
        for copy in keeps:
            copy.wait()


def last_kernel(
    turn,
    me_ref,
    counts_ref,
    own_ref,
    other_ref,
    total_ref,
    inv_ref,
    links_ref,
    base_ref,
    gh_ref,
    held_ref,
    memory_ref,
    w_msg_ref,
    w_in_ref,
    touched_ref,
    nbr_ref,
    codes_ref,
    lists_ref,
    w_nbr_ref,
    w_out_ref,
    rows_ref,
    fresh_kept_ref,
    snap_in_ref,
    emb_out,
    snap_out,
    snap_scr,
    emb_scr,
    sems,
):
    mine = me_ref[0] == turn
    half = own_ref.shape[0]
    events = emb_scr.shape[0]
    rows, touch = memory_ref.shape[0], touched_ref.shape[1]
    snap_store = pltpu.make_async_copy(snap_scr, snap_out, sems.at[0])
    own = jnp.where(mine, own_ref[...], rows_ref[:half, :])
    other = jnp.where(mine, other_ref[...], rows_ref[half:, :])
    near = dot(nbr_ref[:, :half], own) + dot(nbr_ref[:, half:], other)
    hidden = dot(near.astype(BF16), w_nbr_ref[:DM, :]) + dot(codes_ref[...], w_nbr_ref[DM:, :])
    hidden = jnp.maximum(hidden, 0.0).astype(BF16)
    lower = dot(hidden, w_out_ref[DM:, :])
    fresh = updated(
        other_ref[...],
        total_ref[...],
        inv_ref[...],
        links_ref[...],
        base_ref[...],
        gh_ref[...],
        held_ref[...],
        w_msg_ref[DM : 2 * DM, :],
        w_in_ref[...],
    )
    place = pick_rows(rows, touched_ref[turn : turn + 1, :])
    high, low = split_two(fresh)
    snap_scr[...] = memory_ref[...].astype(F32) + (dot(place, high) + dot(place, low))

    @pl.when(mine)
    def _():
        snap_store.start()

    fresh = jnp.where(mine, high, fresh_kept_ref[...])
    block = events // 2
    stores = []
    for i in range(2):
        at = slice(i * block, (i + 1) * block)
        sources = lists_ref[at, 2 * NBRS : 2 * NBRS + 1]
        src_pick = same16(sources, iota((block, touch), 1))
        src_new = dot(src_pick, fresh).astype(BF16)
        out = dot(src_new, w_out_ref[:DM, :]) + lower[at, :]
        live = iota((block, 1), 0) + i * block < counts_ref[me_ref[0]]
        emb_scr[at, :] = jnp.where(live, out, 0.0).astype(BF16)
        store = pltpu.make_async_copy(emb_scr.at[at], emb_out.at[at], sems.at[1 + i])
        store.start()
        stores.append(store)

    @pl.when(mine)
    def _():
        snap_store.wait()

    for store in stores:
        store.wait()


def count_block(lists, number, begin, width):
    lanes = iota((lists.shape[0], width), 1)
    total = same16(lists[:, begin : begin + 1], lanes)
    for q in range(begin + 1, begin + number):
        total += same16(lists[:, q : q + 1], lanes)
    return total


def neighbours_kernel(after_ref, lists_ref, out_ref):
    block = 64

    def step(i, carry):
        at = pl.ds(pl.multiple_of(i * block, block), block)
        out_ref[at, :] = count_block(lists_ref[at, :], NBRS, 0, out_ref.shape[1])
        return carry

    lax.fori_loop(0, out_ref.shape[0] // block, step, 0)


def codes_kernel(after_ref, lists_ref, high_ref, low_ref, out_ref):
    block = 128

    def step(i, carry):
        at = pl.ds(pl.multiple_of(i * block, block), block)
        counts = count_block(lists_ref[at, :], NBRS, NBRS, high_ref.shape[0])
        out_ref[at, :] = (dot(counts, high_ref[...]) + dot(counts, low_ref[...])).astype(BF16)
        return carry

    lax.fori_loop(0, out_ref.shape[0] // block, step, 0)


def tie_kernel(*refs):
    pass


def in_hbm(dims, dtype):
    return pltpu.HBM(dims, dtype)


def stay(arrays):
    return [pltpu.with_memory_space_constraint(x, pltpu.HBM) for x in arrays]


def shape(dims, dtype):
    return jax.ShapeDtypeStruct(dims, dtype)


def params(mib=16):
    return pltpu.CompilerParams(vmem_limit_bytes=mib * 1024 * 1024)


def cost(flops, bytes_accessed):
    return pl.CostEstimate(flops=flops, bytes_accessed=bytes_accessed, transcendentals=0)


def body(
    memory,
    touched,
    src_slot,
    ev_count,
    serve_rows,
    dst_slot,
    nbr_slot,
    ev_gap,
    nbr_gap,
    time_freq,
    time_phase,
    w_msg,
    w_in,
    w_hid,
    w_nbr,
    w_out,
):
    me = lax.axis_index("tm")
    core = me % 2
    sections = lax.axis_size("tm")
    shards = lax.axis_size("node")
    rows = memory.shape[0]
    events = src_slot.shape[2]
    slots = serve_rows.shape[2]
    half = slots // 2
    capacity = slots // shards
    part = capacity // 2
    touched = touched[:, 0, :]
    touch = touched.shape[1]

    lists = [
        serve_rows.reshape(-1, 128),
        dst_slot.reshape(-1, 128),
        src_slot.reshape(-1, 128),
        ev_gap.reshape(-1, 128),
    ]
    lines = sum(x.shape[0] for x in lists) + 4
    packed = pl.pallas_call(
        pack_kernel,
        out_shape=shape((sections, lines, 128), jnp.int32),
        in_specs=[HBM] * 4 + [SMEM],
        out_specs=HBM,
        scratch_shapes=[
            pltpu.VMEM((lines, 128), jnp.int32),
            pltpu.SemaphoreType.DMA((4,)),
            pltpu.SemaphoreType.DMA((sections,)),
        ],
        compiler_params=params(),
        name="pack",
    )(*stay(lists), ev_count)
    everyone = lax.all_to_all(packed, "tm", split_axis=0, concat_axis=0, tiled=True).reshape(
        sections, -1
    )
    serve_all = everyone[:, :slots].reshape(sections, shards, 2, part)
    serve_own = jnp.where(core == 0, serve_all[:, :, 0], serve_all[:, :, 1])
    serve_t = serve_own.reshape(sections, half).T
    at = slots
    dst_all = everyone[:, at : at + events]
    at += events
    src_all = everyone[:, at : at + events]
    at += events
    gap_all = everyone[:, at : at + events]
    at += events
    count_all = everyone[:, at]

    def reordered(slot):
        place = slot % capacity
        mine = (place // part) == core
        return (slot // capacity) * part + place % part + jnp.where(mine, 0, half)

    dst_all = reordered(dst_all)
    touched_t = touched.T
    me_s = me.reshape(1).astype(jnp.int32)
    freq = jnp.pad(time_freq, (0, CODE - TD)).reshape(1, CODE)
    phase = jnp.pad(time_phase, (0, CODE - TD)).reshape(1, CODE)
    w_msg = jnp.pad(w_msg, ((0, CODE - TD), (0, 0)))
    w_nbr = jnp.pad(w_nbr, ((0, CODE - TD), (0, 0)))

    def call(kernel, name, outs, ins, operands, **more):
        return pl.pallas_call(
            kernel,
            out_shape=outs,
            in_specs=ins,
            compiler_params=params(),
            cost_estimate=cost(10**9, 2**22),
            name=name,
            **more,
        )(*operands)

    table, table_low = call(
        table_kernel,
        "table",
        (shape((GAPS, CODE), BF16),) * 2,
        [VMEM] * 2,
        (freq, phase),
        out_specs=(VMEM,) * 2,
    )
    served, memory_now = pl.pallas_call(
        first_serve_kernel,
        out_shape=(shape((half, DM), BF16), shape((rows, DM), BF16)),
        in_specs=[VMEM] * 2 + [ANY] * 4,
        out_specs=(VMEM,) * 2,
        compiler_params=params(),
        name="first_serve",
    )(serve_t, memory, touched, touched_t, table, w_msg)

    def make_links(begin, number, after):
        return call(
            functools.partial(links_kernel, begin),
            "links",
            (
                in_hbm((number, touch, slots), BF16),
                in_hbm((number, touch, DM), BF16),
                in_hbm((number, touch, 128), F32),
                in_hbm((number, rows, 128), BF16),
            ),
            [HBM] + [VMEM] * 3 + [SMEM] + [VMEM] * 3,
            (*stay([after]), src_all, dst_all, gap_all, count_all, table, w_msg, touched),
            out_specs=(
                pl.BlockSpec((1, touch, slots), lambda t: (t, 0, 0)),
                pl.BlockSpec((1, touch, DM), lambda t: (t, 0, 0)),
                pl.BlockSpec((1, touch, 128), lambda t: (t, 0, 0)),
                pl.BlockSpec((1, rows, 128), lambda t: (t, 0, 0)),
            ),
            grid=(number,),
        )

    split = min(FIRST, sections)
    parts = [make_links(0, split, memory)]
    lists_t = jnp.concatenate(
        [reordered(nbr_slot[0, 0]), nbr_gap[0, 0], src_slot.reshape(1, events)], axis=0
    ).T
    snap, keeps = (), ()
    swap = [(i, i ^ 1) for i in range(sections)]
    for turn in range(sections):
        own = lax.all_to_all(
            served.reshape(shards, part, DM), "node", split_axis=0, concat_axis=0, tiled=True
        ).reshape(half, DM)
        if turn == 1:
            nbr_counts = call(
                neighbours_kernel,
                "neighbour_counts",
                in_hbm((events, slots), BF16),
                [HBM, VMEM],
                (*stay([memory_now]), lists_t),
                out_specs=VMEM,
            )
            nbr_codes = call(
                codes_kernel,
                "codes",
                in_hbm((events, CODE), BF16),
                [HBM] + [VMEM] * 3,
                (*stay([memory_now]), lists_t, table, table_low),
                out_specs=VMEM,
            )
            parts.append(make_links(split, sections - split, memory_now))
        if turn < 2:
            beside = stay([parts[0][0]] if turn == 0 else [nbr_counts, nbr_codes, parts[1][0]])
            own = pl.pallas_call(
                tie_kernel,
                out_shape=shape(own.shape, own.dtype),
                in_specs=[ANY] + [HBM] * len(beside),
                out_specs=ANY,
                input_output_aliases={0: 0},
                compiler_params=params(1),
                name="tie",
            )(own, *beside)
        other = lax.ppermute(own, "tm", swap)
        late_links = turn >= split
        outs = call(
            functools.partial(ready_kernel, turn, turn - split * late_links),
            "ready",
            (
                shape((touch, DM), F32),
                shape((touch, 128), F32),
                shape((touch, half), BF16),
                shape((touch, DM), F32),
                shape((touch, 3 * DM), F32),
                shape((touch, DM), BF16),
                shape((rows, DM), BF16),
            )
            + (in_hbm((rows, DM), F32),) * (turn > 0),
            [SMEM] + [VMEM] * 6 + [HBM] * (4 + len(snap)),
            (
                me_s,
                own,
                memory_now,
                touched,
                touched_t,
                w_msg,
                w_hid,
                *stay((*parts[late_links], *snap)),
            ),
            out_specs=(VMEM,) * 7 + (HBM,) * (turn > 0),
            scratch_shapes=[
                pltpu.VMEM((touch, half), BF16),
                pltpu.VMEM((touch, DM), BF16),
                pltpu.VMEM((rows, 128), BF16),
                pltpu.VMEM((rows, DM), F32),
                pltpu.SemaphoreType.DMA((5,)),
                pltpu.SemaphoreType.DMA,
            ],
            input_output_aliases={11: 7} if snap else {},
        )
        ready, snap = outs[:7], outs[7:]
        if turn + 1 == sections:
            break
        memory_now, served, *keeps = call(
            functools.partial(update_kernel, turn),
            "update",
            (
                (in_hbm if turn == 0 else shape)((rows, DM), BF16),
                shape((half, DM), BF16),
                in_hbm((slots, DM), BF16),
                in_hbm((touch, DM), BF16),
            ),
            [SMEM] + [VMEM] * 13 + [HBM] * len(keeps),
            (me_s, own, other, *ready, touched, serve_t, w_msg, w_in, *stay(keeps)),
            out_specs=(VMEM,) * 2 + (HBM,) * 2,
            scratch_shapes=[pltpu.VMEM((touch, DM), BF16), pltpu.SemaphoreType.DMA((3,))],
            input_output_aliases={14: 2, 15: 3} if keeps else {},
        )
    late = (nbr_counts, nbr_codes, lists_t, w_nbr, w_out)
    emb, snap = call(
        functools.partial(last_kernel, turn),
        "last",
        (in_hbm((events, DM), BF16), in_hbm((rows, DM), F32)),
        [SMEM] * 2 + [VMEM] * 19 + [HBM],
        (
            me_s,
            count_all,
            own,
            other,
            *ready,
            w_msg,
            w_in,
            touched,
            *late,
            *keeps,
            *stay(snap),
        ),
        out_specs=(HBM,) * 2,
        scratch_shapes=[
            pltpu.VMEM((rows, DM), F32),
            pltpu.VMEM((events, DM), BF16),
            pltpu.SemaphoreType.DMA((3,)),
        ],
        input_output_aliases={21: 1},
    )
    return (emb[None, None], snap[None])


def solution(mesh):
    return jax.shard_map(
        body,
        mesh=mesh,
        in_specs=(
            P("node", None),
            P(None, "node", None),
            P("tm", "node", None),
            P("tm", "node"),
            P("tm", "node", None),
            P("tm", "node", None),
            P("tm", "node", None, None),
            P("tm", "node", None),
            P("tm", "node", None, None),
            P(),
            P(),
            P(),
            P(),
            P(),
            P(),
            P(),
        ),
        out_specs=(P("tm", "node", None, None), P("tm", "node", None)),
        check_vma=False,
    )
```
